32 devices in a mesh: grp: 2 (over y), pas: 4 (over x, core), fsdp: 4 (over z).
Axes of the slice: x: 2, y: 2, z: 4, core: 2. Of those that a mesh axis runs over, the one named last changes fastest.
Arguments:
- passages: bfloat16 [32, 128, 4096], P(('grp', 'pas'), None, 'fsdp'), parts along dimension 0, may hold values from -3 to 3
- cotangent: bfloat16 [32, 128, 4096], P(('grp', 'pas'), None, 'fsdp'), parts along dimension 0, may hold values from -6 to 6
- passage_counts: int32 [8], P(('grp', 'pas')), parts along dimension 0, may hold values from 1 to 4, 8 in all
- norm_gain: float32 [4096], replicated, may hold values from 0.1 to 1.9
- w_query: bfloat16 [4096, 4096], P('pas', 'fsdp'), may hold values from -0.25 to 0.25
- w_key: bfloat16 [4096, 4096], P('pas', 'fsdp')
- w_value: bfloat16 [4096, 4096], P('pas', 'fsdp'), may hold values from -0.09375 to 0.09375
- w_out: bfloat16 [4096, 4096], P('fsdp', 'pas'), may hold values from -0.29882812 to 0.29882812
Outputs:
- encoded: bfloat16 [32, 128, 4096], P(('grp', 'pas'), None, 'fsdp'), parts along dimension 0
- input_grad: bfloat16 [32, 128, 4096], P(('grp', 'pas'), None, 'fsdp'), parts along dimension 0
- gain_grad: float32 [8192], P(('grp', 'fsdp')), parts along dimension 0
The draws below stay inside these ranges and needn't reach their ends.
There are 2 independent parts, one for each index of `grp`. The reference program is written for one: setup_inputs(seed, part) draws one part's arguments, and reference() takes and returns one part's arrays. A program takes and returns all parts, laid end to end along the dimension named above; an argument that names none is the same for every part. Nothing has to cross between parts.
Inputs may be any that keep to these rules, and one draw needn't show every extreme that they name: `passage_counts`: counts are 1 or more; the 4 counts of a group sum to 8, and one of them equals 4.
All inputs are finite; a program needn't handle non-finite values.
Results may differ from the reference program's by a relative error of at most 0.012.
Values may be sent and summed in bfloat16 or wider, within the bound.
No kernel may reach another device: no remote copies, remote signals or barrier semaphores. Data moves between devices by JAX's collectives and lax.ppermute only.
A program may use at most 128 MiB of HBM per device.

```python
import math
import jax
import jax.numpy as jnp
import numpy as np
from jax import lax

D = 4096
HEADS = 64
HD = 64
LEN = 128
BAL = 2
OWN = 4
SLOTS = 16
N_PAS = 4
N_FSDP = 4


def common_base(key):
    return jax.random.normal(key, (D, HEADS * HD), jnp.float32) / math.sqrt(D)


def draw_w_key(key, part):
    base = common_base(key)
    return base.astype(jnp.bfloat16)


def draw_w_query(key, part):
    key = jax.random.fold_in(key, 7)
    second_key = jax.random.fold_in(key, 1)
    drawn = jax.random.normal(second_key, (D, HEADS * HD), jnp.float32) / math.sqrt(D * HD)
    return jnp.clip(drawn, -0.25, 0.25).astype(jnp.bfloat16)


def shard_levels(stream_key, dims, shards, smallest, largest):
    loudness, own = 1.0, jax.random.fold_in(stream_key, 6)
    for axis_at, blocks in shards:
        heights = jnp.exp(jax.random.uniform(jax.random.fold_in(own, axis_at), (blocks,), jnp.float32, smallest / len(shards), largest / len(shards)))
        loudness = loudness * jnp.repeat(heights, dims[axis_at] // blocks).reshape([-1 if axis == axis_at else 1 for axis in range(len(dims))])
    return loudness


def length_profile(count, total, limit, lean):
    loads = [(1 << 20) // math.isqrt(standing ** lean) + 1 for standing in range(2, count + 1)]
    surplus, holding = total - limit - (count - 1), [1] * (count - 1)
    while surplus > 0:
        free = [i for i in range(count - 1) if holding[i] < limit]
        whole, remaining = sum([loads[i] for i in free]), surplus
        for i in free:
            extra = min(limit - holding[i], max(1, remaining * loads[i] // whole), surplus)
            holding[i] = holding[i] + extra
            surplus = surplus - extra
    return np.array([limit] + holding)


def uneven_parts(key, amount, total, reach, skew):
    if amount == 2:
        one = jax.random.randint(key, (), max(1, total - reach), min(reach, total - 1) + 1)
        return jnp.stack([one, total - one])
    sizes = jnp.asarray(length_profile(amount, total, reach, skew), jnp.int32)
    pairs = (amount - 1) // 2
    donor, receiver = sizes[1:1 + 2 * pairs:2], sizes[2:2 + 2 * pairs:2]
    room = jnp.minimum(donor - 1, reach - receiver)
    passed = jax.random.randint(jax.random.fold_in(key, 1), (pairs,), 0, 1 << 20) % (room + 1)
    sizes = sizes.at[1:1 + 2 * pairs:2].set(donor - passed).at[2:2 + 2 * pairs:2].set(receiver + passed)
    return sizes[jax.random.permutation(jax.random.fold_in(key, 2), amount)]


def normal_values(key, shape, scale, limit, shards=(), held_as=jnp.bfloat16):
    result = scale * jax.random.normal(key, shape, jnp.float32)
    if shards:
        result = result * shard_levels(key, shape, shards, -0.22, 0.18)
    return jnp.clip(result, -limit, limit).astype(held_as)


def setup_inputs(seed: int = 0, part: int = 0) -> dict:
    seeds = jax.random.split(jax.random.key(seed), 9)
    part_splits = jax.random.split(jax.random.fold_in(seeds[8], part), 9)
    passages = normal_values(part_splits[0], (SLOTS, LEN, D), 0.5, 3.0, ((0, 4), (2, 4)))
    cotangent = normal_values(part_splits[1], (SLOTS, LEN, D), 1.0, 6.0, ((0, 4), (2, 4)))
    passage_counts = uneven_parts(part_splits[2], N_PAS, BAL * N_PAS, OWN, 2).astype(jnp.int32)
    norm_gain = jnp.clip(1.0 + 0.18 * jax.random.normal(seeds[3], (D,), jnp.float32), 0.1, 1.9)
    w_query = draw_w_query(jax.random.fold_in(seeds[8], 71), part)
    w_key = draw_w_key(jax.random.fold_in(seeds[8], 71), part)
    w_value = normal_values(seeds[6], (D, HEADS * HD), D ** -0.5, 0.09375, ((0, 4), (1, 4)))
    w_out = normal_values(seeds[7], (HEADS * HD, D), 0.05, 0.29882812, ((0, 4), (1, 4)))
    return dict(passages=passages, cotangent=cotangent, passage_counts=passage_counts, norm_gain=norm_gain, w_query=w_query, w_key=w_key, w_value=w_value, w_out=w_out)


EPSILON = 1e-06

def reference(passages, cotangent, passage_counts, norm_gain, w_query, w_key, w_value, w_out):
    counts = passage_counts.astype(jnp.int32)
    first_rank = (jnp.cumsum(counts) - counts).astype(jnp.int32)
    rank_ids = jnp.arange(N_PAS * BAL, dtype=jnp.int32)
    owner = (lax.optimization_barrier(jnp.sum((first_rank[None, :] <= rank_ids[:, None]).astype(jnp.int32), axis=1)) - 1).astype(jnp.int32)
    slot_ids = (owner * OWN + rank_ids - first_rank[owner]).astype(jnp.int32)
    tokens_live = passages[slot_ids]
    grads_live = cotangent[slot_ids]
    group_cols = HEADS * HD // N_FSDP

    def encode_one(pair_rows):
        tokens, upstream = pair_rows
        tokens_f32 = tokens.astype(jnp.float32)
        inverse = lax.rsqrt(lax.optimization_barrier(jnp.mean(tokens_f32 * tokens_f32, axis=-1, keepdims=True)) + EPSILON)
        unit_rows = tokens_f32 * inverse
        normed = (unit_rows * norm_gain).astype(jnp.bfloat16)
        query = jnp.dot(normed, w_query, preferred_element_type=jnp.float32).astype(jnp.bfloat16)
        keys = jnp.dot(normed, w_key, preferred_element_type=jnp.float32).astype(jnp.bfloat16)
        values = jnp.dot(normed, w_value, preferred_element_type=jnp.float32).astype(jnp.bfloat16)
        query_h = query.reshape(LEN, HEADS, HD).astype(jnp.float32)
        keys_h = keys.reshape(LEN, HEADS, HD).astype(jnp.float32)
        values_h = values.reshape(LEN, HEADS, HD).astype(jnp.float32)
        scores = jnp.einsum('lhe,mhe->hlm', query_h, keys_h)
        probs = jax.nn.softmax(scores, axis=-1)
        probs_low = probs.astype(jnp.bfloat16).astype(jnp.float32)
        context = jnp.einsum('hlm,mhe->lhe', probs_low, values_h).astype(jnp.bfloat16)
        context_groups = context.reshape(LEN, N_FSDP, group_cols).astype(jnp.float32)
        out_groups = w_out.reshape(N_FSDP, group_cols, D).astype(jnp.float32)
        parts = jnp.einsum('lgc,gcd->lgd', context_groups, out_groups)
        parts_low = lax.optimization_barrier(parts.astype(jnp.bfloat16))
        attention = lax.optimization_barrier(jnp.sum(parts_low.astype(jnp.float32), axis=1))
        encoded_rows = (tokens_f32 + attention).astype(jnp.bfloat16)
        w_out_t = jnp.transpose(w_out)
        d_context = jnp.dot(upstream, w_out_t, preferred_element_type=jnp.float32).astype(jnp.bfloat16)
        d_context_h = d_context.reshape(LEN, HEADS, HD).astype(jnp.float32)
        d_values = jnp.einsum('hlm,lhe->mhe', probs_low, d_context_h).astype(jnp.bfloat16)
        d_probs = jnp.einsum('lhe,mhe->hlm', d_context_h, values_h)
        d_scores = (probs * (d_probs - lax.optimization_barrier(jnp.sum(d_probs * probs, axis=-1, keepdims=True)))).astype(jnp.bfloat16)
        d_scores_f = d_scores.astype(jnp.float32)
        d_query = jnp.einsum('hlm,mhe->lhe', d_scores_f, keys_h).astype(jnp.bfloat16)
        d_keys = jnp.einsum('hlm,lhe->mhe', d_scores_f, query_h).astype(jnp.bfloat16)

        def group_back(grad, weight):
            grad_groups = grad.reshape(LEN, N_FSDP, group_cols).astype(jnp.float32)
            weight_groups = weight.reshape(D, N_FSDP, group_cols).astype(jnp.float32)
            return jnp.einsum('lgc,dgc->lgd', grad_groups, weight_groups)
        back_parts = group_back(d_query, w_query) + group_back(d_keys, w_key) + group_back(d_values, w_value)
        back_low = lax.optimization_barrier(back_parts.astype(jnp.bfloat16))
        d_normed = lax.optimization_barrier(jnp.sum(back_low.astype(jnp.float32), axis=1))
        d_unit = d_normed * norm_gain
        d_tokens = inverse * (d_unit - unit_rows * lax.optimization_barrier(jnp.mean(d_unit * unit_rows, axis=-1, keepdims=True)))
        grad_rows = (upstream.astype(jnp.float32) + d_tokens).astype(jnp.bfloat16)
        gain_term = lax.optimization_barrier(jnp.sum(d_normed * unit_rows, axis=0))
        return (encoded_rows, grad_rows, gain_term)
    encoded_live, grads_out, gain_terms = lax.map(encode_one, (tokens_live, grads_live))
    encoded = jnp.zeros(passages.shape, jnp.bfloat16).at[slot_ids].set(encoded_live)
    input_grad = jnp.zeros(passages.shape, jnp.bfloat16).at[slot_ids].set(grads_out)
    gain_grad = lax.optimization_barrier(jnp.sum(gain_terms, axis=0))
    return (encoded, input_grad, gain_grad)
```

```python
import jax
import jax.numpy as jnp
from jax import lax
from jax.experimental import pallas as pl
from jax.experimental.pallas import tpu as pltpu
from jax.sharding import PartitionSpec as P

HD = 64
BAL = 2
EPSILON = 1e-06
VMEM_LIMIT = 50 * 2**20


def entering(shard, axis, combine, identity):
    length, position = (lax.axis_size(axis), lax.axis_index(axis))
    everything = lax.all_gather(shard, axis)
    start = jnp.broadcast_to(jnp.asarray(identity, shard.dtype), shard.shape)

    def lap(k, before):
        reached = k < position
        new = combine(before, everything[k])
        return jnp.where(reached, new, before)

    return lax.fori_loop(0, length, lap, start)


def add_counts(earlier, later):
    return earlier + later


def general_body(passages, cotangent, passage_counts, norm_gain, w_query, w_key, w_value, w_out):
    peer_total = lax.axis_size("pas")
    slots, seq_len, part_width = passages.shape
    flat_width = seq_len * part_width
    own_count = passage_counts[0]
    first_rank = entering(passage_counts, "pas", add_counts, jnp.zeros_like(passage_counts))[0]
    slot_index = jnp.arange(slots, dtype=jnp.int32)
    slot_rank = first_rank + slot_index
    is_live = slot_index < own_count
    peer_index = jnp.arange(peer_total, dtype=jnp.int32)
    routing_mask = is_live[None, :] & ((slot_rank % peer_total)[None, :] == peer_index[:, None])
    routing = routing_mask.astype(jnp.bfloat16)
    sent_rank = jnp.max(jnp.where(routing_mask, slot_rank[None, :], -1), axis=1).astype(jnp.int32)
    send_tokens = jnp.dot(
        routing, passages.reshape(slots, flat_width), preferred_element_type=jnp.float32
    ).astype(jnp.bfloat16)
    send_grads = jnp.dot(
        routing, cotangent.reshape(slots, flat_width), preferred_element_type=jnp.float32
    ).astype(jnp.bfloat16)
    got_tokens, got_grads, got_rank = (
        lax.all_to_all(send_tokens, "pas", split_axis=0, concat_axis=0, tiled=True),
        lax.all_to_all(send_grads, "pas", split_axis=0, concat_axis=0, tiled=True),
        lax.all_to_all(sent_rank, "pas", split_axis=0, concat_axis=0, tiled=True),
    )
    picked_mask = (got_rank[None, :] >= 0) & (
        got_rank[None, :] // peer_total == jnp.arange(BAL, dtype=jnp.int32)[:, None]
    )
    picked = picked_mask.astype(jnp.bfloat16)
    returned = jnp.transpose(picked)
    local_tokens = (
        jnp.dot(picked, got_tokens, preferred_element_type=jnp.float32)
        .astype(jnp.bfloat16)
        .reshape(BAL, seq_len, part_width)
    )
    local_grads = (
        jnp.dot(picked, got_grads, preferred_element_type=jnp.float32)
        .astype(jnp.bfloat16)
        .reshape(BAL, seq_len, part_width)
    )
    query_w, key_w, value_w, out_w = (
        lax.all_gather(w_query, "pas", axis=0, tiled=True),
        lax.all_gather(w_key, "pas", axis=0, tiled=True),
        lax.all_gather(w_value, "pas", axis=0, tiled=True),
        lax.all_gather(w_out, "pas", axis=1, tiled=True),
    )
    full_tokens = lax.all_gather(local_tokens, "fsdp", axis=2, tiled=True)
    width = full_tokens.shape[2]
    feature_start = lax.axis_index("fsdp") * part_width
    full_f32 = full_tokens.astype(jnp.float32)
    inverse = lax.rsqrt(jnp.mean(full_f32 * full_f32, axis=-1, keepdims=True) + EPSILON)
    unit_rows = full_f32 * inverse
    normed = (unit_rows * norm_gain).astype(jnp.bfloat16)
    local_cols = query_w.shape[1]
    head_count = local_cols // HD
    flat_rows = normed.reshape(BAL * seq_len, width)

    def project(weight):
        result = jnp.dot(flat_rows, weight, preferred_element_type=jnp.float32).astype(jnp.bfloat16)
        return result.reshape(BAL, seq_len, head_count, HD)

    query = project(query_w)
    keys = project(key_w)
    values = project(value_w)
    scores = jnp.einsum("blhe,bmhe->bhlm", query, keys, preferred_element_type=jnp.float32)
    probs = jax.nn.softmax(scores, axis=-1)
    probs_low = probs.astype(jnp.bfloat16)
    context = jnp.einsum(
        "bhlm,bmhe->blhe", probs_low, values, preferred_element_type=jnp.float32
    ).astype(jnp.bfloat16)
    context_rows = context.reshape(BAL * seq_len, local_cols)
    partial_out = jnp.dot(context_rows, out_w, preferred_element_type=jnp.float32).reshape(
        BAL, seq_len, width
    )
    attention = lax.psum_scatter(
        partial_out.astype(jnp.bfloat16), "fsdp", scatter_dimension=2, tiled=True
    ).astype(jnp.float32)
    states = (local_tokens.astype(jnp.float32) + attention).astype(jnp.bfloat16)
    states_back = jnp.dot(
        returned, states.reshape(BAL, flat_width), preferred_element_type=jnp.float32
    ).astype(jnp.bfloat16)
    states_home = lax.all_to_all(states_back, "pas", split_axis=0, concat_axis=0, tiled=True)
    upstream_rows = lax.all_gather(local_grads, "fsdp", axis=2, tiled=True).reshape(
        BAL * seq_len, width
    )
    d_context = jnp.einsum(
        "td,cd->tc", upstream_rows, out_w, preferred_element_type=jnp.float32
    ).astype(jnp.bfloat16)
    d_context = d_context.reshape(BAL, seq_len, head_count, HD)
    d_values = jnp.einsum(
        "bhlm,blhe->bmhe", probs_low, d_context, preferred_element_type=jnp.float32
    ).astype(jnp.bfloat16)
    d_probs = jnp.einsum("blhe,bmhe->bhlm", d_context, values, preferred_element_type=jnp.float32)
    d_scores = (probs * (d_probs - jnp.sum(d_probs * probs, axis=-1, keepdims=True))).astype(
        jnp.bfloat16
    )
    d_query = jnp.einsum(
        "bhlm,bmhe->blhe", d_scores, keys, preferred_element_type=jnp.float32
    ).astype(jnp.bfloat16)
    d_keys = jnp.einsum(
        "bhlm,blhe->bmhe", d_scores, query, preferred_element_type=jnp.float32
    ).astype(jnp.bfloat16)

    def back_project(grad, weight):
        grad_rows = grad.reshape(BAL * seq_len, local_cols)
        return jnp.einsum("tc,dc->td", grad_rows, weight, preferred_element_type=jnp.float32)

    d_normed = (
        back_project(d_query, query_w)
        + back_project(d_keys, key_w)
        + back_project(d_values, value_w)
    )
    d_normed_part = lax.psum_scatter(
        d_normed.reshape(BAL, seq_len, width).astype(jnp.bfloat16),
        "fsdp",
        scatter_dimension=2,
        tiled=True,
    ).astype(jnp.float32)
    unit_part = lax.dynamic_slice_in_dim(unit_rows, feature_start, part_width, 2)
    gain_part = lax.dynamic_slice_in_dim(norm_gain, feature_start, part_width, 0)
    d_unit = d_normed_part * gain_part
    row_total = lax.psum(jnp.sum(d_unit * unit_part, axis=-1, keepdims=True), "fsdp")
    row_mean = row_total / width
    d_tokens = inverse * (d_unit - unit_part * row_mean)
    grads_local = (local_grads.astype(jnp.float32) + d_tokens).astype(jnp.bfloat16)
    gain_grad = lax.psum(jnp.sum(d_normed_part * unit_part, axis=(0, 1)), "pas")
    grads_back = jnp.dot(
        returned, grads_local.reshape(BAL, flat_width), preferred_element_type=jnp.float32
    ).astype(jnp.bfloat16)
    grads_home = lax.all_to_all(grads_back, "pas", split_axis=0, concat_axis=0, tiled=True)
    routing_back = jnp.transpose(routing)
    encoded = (
        jnp.dot(routing_back, states_home, preferred_element_type=jnp.float32)
        .astype(jnp.bfloat16)
        .reshape(slots, seq_len, part_width)
    )
    input_grad = (
        jnp.dot(routing_back, grads_home, preferred_element_type=jnp.float32)
        .astype(jnp.bfloat16)
        .reshape(slots, seq_len, part_width)
    )
    return (encoded, input_grad, gain_grad)


def swap(array, axis, bit):
    return lax.ppermute(array, axis, [(i, i ^ bit) for i in range(lax.axis_size(axis))])


def dot_nn(a, b):
    return jnp.dot(a, b, preferred_element_type=jnp.float32)


def dot_nt(a, b):
    return lax.dot_general(a, b, (((1,), (1,)), ((), ())), preferred_element_type=jnp.float32)


def dot_tn(a, b):
    return lax.dot_general(a, b, (((0,), (0,)), ((), ())), preferred_element_type=jnp.float32)


def halves(at):
    first = pl.multiple_of(at * 512, 512)
    second = pl.multiple_of((1 - at) * 512, 512)
    return pl.ds(first, 512), pl.ds(second, 512)


def project_kernel(pos, rows, own, core, xh, yh, xch, ych, out):
    b = pos[0]
    near, far = halves(pos[1])
    total = dot_nn(rows[b], own[...]) + dot_nn(rows[b ^ 1], core[...])
    total += dot_nn(rows[b ^ 2, :, near], xh[...]) + dot_nn(rows[b ^ 2, :, far], yh[...])
    total += dot_nn(rows[b ^ 3, :, near], xch[...]) + dot_nn(rows[b ^ 3, :, far], ych[...])
    out[...] = total.astype(out.dtype)


def project_out_kernel(pos, rows, own, core, xh, yh, xch, ych, out):
    b = pos[0]
    near, far = halves(pos[1])
    total = dot_nt(rows[b], own[...]) + dot_nt(rows[b ^ 1], core[...])
    total += dot_nt(rows[b ^ 2, :, near], xh[...]) + dot_nt(rows[b ^ 2, :, far], yh[...])
    total += dot_nt(rows[b ^ 3, :, near], xch[...]) + dot_nt(rows[b ^ 3, :, far], ych[...])
    out[...] = total.astype(out.dtype)


def half_at(at, step):
    return pl.ds(pl.multiple_of(at * 512 + step * 128, 128), 128)


def emit_kernel(pos, ctx, own, core, xh, yh, xch, ych, out):
    b = pos[0]
    step = pl.program_id(0)
    whole = pl.ds(pl.multiple_of(step * 256, 256), 256)
    near, far = half_at(pos[1], step), half_at(1 - pos[1], step)
    rows = ctx[...]
    out[b, :, whole] = dot_nn(rows, own[...]).astype(out.dtype)
    out[b ^ 1, :, whole] = dot_nn(rows, core[...]).astype(out.dtype)
    two = dot_nn(rows, jnp.concatenate([xh[...], yh[...]], axis=1)).astype(out.dtype)
    out[b ^ 2, :, near] = two[:, :128]
    out[b ^ 2, :, far] = two[:, 128:]
    two = dot_nn(rows, jnp.concatenate([xch[...], ych[...]], axis=1)).astype(out.dtype)
    out[b ^ 3, :, near] = two[:, :128]
    out[b ^ 3, :, far] = two[:, 128:]


def back_kernel(pos, dq, dk, dv, *refs):
    weights, out = refs[:18], refs[18]
    b = pos[0]
    step = pl.program_id(0)
    whole = pl.ds(pl.multiple_of(step * 256, 256), 256)
    near, far = half_at(pos[1], step), half_at(1 - pos[1], step)
    grads = (dq[...], dk[...], dv[...])

    def total(pick):
        return sum(dot_nt(g, pick(weights[6 * i : 6 * i + 6])) for i, g in enumerate(grads))

    out[b, :, whole] = total(lambda w: w[0][...]).astype(out.dtype)
    out[b ^ 1, :, whole] = total(lambda w: w[1][...]).astype(out.dtype)
    two = total(lambda w: jnp.concatenate([w[2][...], w[3][...]], axis=0)).astype(out.dtype)
    out[b ^ 2, :, near] = two[:, :128]
    out[b ^ 2, :, far] = two[:, 128:]
    two = total(lambda w: jnp.concatenate([w[4][...], w[5][...]], axis=0)).astype(out.dtype)
    out[b ^ 3, :, near] = two[:, :128]
    out[b ^ 3, :, far] = two[:, 128:]


def attention_kernel(q_ref, k_ref, v_ref, dc_ref, ctx_ref, dq_ref, dk_ref, dv_ref):
    seq = q_ref.shape[0]
    lane = lax.broadcasted_iota(jnp.int32, (seq, 128), 1)
    first = lane < HD
    mask0 = jnp.where(first, 1.0, 0.0).astype(jnp.bfloat16)
    mask1 = jnp.where(first, 0.0, 1.0).astype(jnp.bfloat16)
    for pair in range(q_ref.shape[1] // 128):
        at = pl.ds(pair * 128, 128)
        q, k, v, dc = q_ref[:, at], k_ref[:, at], v_ref[:, at], dc_ref[:, at]
        keys = jnp.concatenate([k * mask0, k * mask1], axis=0)
        values = jnp.concatenate([v * mask0, v * mask1], axis=0)
        scores = dot_nt(q, keys)
        d_probs = dot_nt(dc, values)
        probs, d_scores = [], []
        for h in range(2):
            s = scores[:, h * seq : (h + 1) * seq]
            dp = d_probs[:, h * seq : (h + 1) * seq]
            e = jnp.exp(s - jnp.max(s, axis=-1, keepdims=True))
            p = e / jnp.sum(e, axis=-1, keepdims=True)
            ds = p * (dp - jnp.sum(dp * p, axis=-1, keepdims=True))
            probs.append(p.astype(jnp.bfloat16))
            d_scores.append(ds.astype(jnp.bfloat16))
        low = jnp.concatenate(probs, axis=1)
        ds = jnp.concatenate(d_scores, axis=1)
        ctx_ref[:, at] = dot_nn(low, values).astype(jnp.bfloat16)
        dq_ref[:, at] = dot_nn(ds, keys).astype(jnp.bfloat16)
        both = dot_tn(low, dc)
        dv_ref[:, at] = jnp.where(first, both[:seq], both[seq:]).astype(jnp.bfloat16)
        both = dot_tn(ds, q)
        dk_ref[:, at] = jnp.where(first, both[:seq], both[seq:]).astype(jnp.bfloat16)


def whole_spec(array):
    zeros = (0,) * array.ndim
    return pl.BlockSpec(array.shape, lambda j, pos: zeros)


def call(kernel, pos, rows, pieces, tile, out_shape, out_tile):
    def cut(array):
        shape = list(array.shape)
        shape[tile] //= 4
        return pl.BlockSpec(tuple(shape), lambda j, pos: (j, 0) if tile == 0 else (0, j))

    flops = 2 * 256 * sum(p.size for p in pieces)
    size = 2 * sum(p.size for p in pieces)
    return pl.pallas_call(
        kernel,
        grid_spec=pltpu.PrefetchScalarGridSpec(
            num_scalar_prefetch=1,
            grid=(4,),
            in_specs=[whole_spec(r) for r in rows] + [cut(p) for p in pieces],
            out_specs=out_tile,
        ),
        out_shape=out_shape,
        cost_estimate=pl.CostEstimate(flops=flops, bytes_accessed=size, transcendentals=0),
        compiler_params=pltpu.CompilerParams(vmem_limit_bytes=VMEM_LIMIT),
    )(pos, *rows, *pieces)


def attend(query, keys, values, d_context):
    rows, cols = query.shape
    spec = pl.BlockSpec((rows // BAL, cols // 2), lambda i, j: (i, j))
    shape = jax.ShapeDtypeStruct(query.shape, jnp.bfloat16)
    return pl.pallas_call(
        attention_kernel,
        grid=(BAL, 2),
        in_specs=[spec] * 4,
        out_specs=[spec] * 4,
        out_shape=[shape] * 4,
        cost_estimate=pl.CostEstimate(
            flops=32 * 12 * 128 * 128 * 128, bytes_accessed=8 * 2 * query.size, transcendentals=2**19
        ),
        compiler_params=pltpu.CompilerParams(vmem_limit_bytes=VMEM_LIMIT),
    )(query, keys, values, d_context)


def fetch_weight(weight, group, axis):
    half = lax.dynamic_slice_in_dim(weight, group * 512, 512, axis)
    core = swap(weight, "pas", 1)
    xh = swap(half, "pas", 2)
    yh = swap(xh, "grp", 1)
    xch = swap(xh, "pas", 1)
    ych = swap(yh, "pas", 1)
    return [weight, core, xh, yh, xch, ych]


def fast_body(passages, cotangent, passage_counts, norm_gain, w_query, w_key, w_value, w_out):
    me = lax.axis_index("pas")
    group = lax.axis_index("grp")
    feature = lax.axis_index("fsdp")
    seq = passages.shape[1]
    pos = jnp.stack([me, group]).astype(jnp.int32)

    counts = lax.all_gather(passage_counts, "pas", axis=0, tiled=True)
    index = jnp.arange(4, dtype=jnp.int32)
    single = counts == 1
    source = jnp.sum(jnp.where(counts == 4, index, 0))
    rank = lambda d: jnp.minimum(jnp.sum((single & (index < d)).astype(jnp.int32)), 1)
    host0 = jnp.min(jnp.where(single, index, 4))
    host1 = jnp.max(jnp.where(single, index, -1))
    own_count = passage_counts[0]
    relation = me ^ source

    def second(array):
        extra = array[2:4]
        extra_core = swap(extra, "pas", 1)
        there = rank(me ^ 2)
        picked = jnp.where(source == me, extra, extra_core)
        sent = jnp.where(there == 0, picked[0], picked[1])
        got_x = swap(sent, "pas", 2)
        from_core = jnp.where(rank(me) == 0, extra_core[0], extra_core[1])
        foreign = jnp.where(relation == 1, from_core, got_x)
        return jnp.where(own_count >= 2, array[1], foreign)

    tokens = jnp.concatenate([passages[0], second(passages)], axis=0)
    grads = jnp.concatenate([cotangent[0], second(cotangent)], axis=0)

    key_w = fetch_weight(w_key, group, 0)
    query_w = fetch_weight(w_query, group, 0)
    value_w = fetch_weight(w_value, group, 0)
    out_w = fetch_weight(w_out, group, 1)

    all_tokens = lax.all_gather(tokens, "fsdp", axis=0)
    all_grads = lax.all_gather(grads, "fsdp", axis=0)

    tokens_f32 = all_tokens.astype(jnp.float32)
    width = norm_gain.shape[0]
    gain = norm_gain.reshape(4, 1, 1024)
    inverse = lax.rsqrt(
        jnp.sum(tokens_f32 * tokens_f32, axis=(0, 2), keepdims=True) / width + EPSILON
    )
    normed = (tokens_f32 * inverse * gain).astype(jnp.bfloat16)

    rows_shape = jax.ShapeDtypeStruct((2 * seq, 1024), jnp.bfloat16)
    rows_tile = pl.BlockSpec((2 * seq, 256), lambda j, pos: (0, j))
    wide_shape = jax.ShapeDtypeStruct((4, 2 * seq, 1024), jnp.bfloat16)
    wide_tile = pl.BlockSpec((4, 2 * seq, 1024), lambda j, pos: (0, 0, 0))

    def project(pieces):
        return call(project_kernel, pos, [normed], pieces, 1, rows_shape, rows_tile)

    keys = project(key_w)
    query = project(query_w)
    values = project(value_w)
    d_context = call(project_out_kernel, pos, [all_grads], out_w, 0, rows_shape, rows_tile)
    context, d_query, d_keys, d_values = attend(query, keys, values, d_context)
    d_normed = call(
        back_kernel, pos, [d_query, d_keys, d_values], query_w + key_w + value_w, 0, wide_shape, wide_tile
    )
    partial_out = call(emit_kernel, pos, [context], out_w, 1, wide_shape, wide_tile)

    d_part = lax.psum_scatter(d_normed, "fsdp", scatter_dimension=0).astype(jnp.float32)
    attention = lax.psum_scatter(partial_out, "fsdp", scatter_dimension=0).astype(jnp.float32)

    row_total = jnp.sum(
        d_normed.astype(jnp.float32) * gain * (tokens_f32 * inverse), axis=(0, 2)
    ).reshape(2, seq)
    row_total += swap(row_total, "fsdp", 1)
    row_total += swap(row_total, "fsdp", 2)
    row_mean = row_total.reshape(2 * seq, 1) / width

    gain_part = lax.dynamic_slice_in_dim(norm_gain, feature * 1024, 1024, 0)
    inverse_rows = inverse.reshape(2 * seq, 1)
    unit_part = tokens.astype(jnp.float32) * inverse_rows
    d_tokens = inverse_rows * (d_part * gain_part - unit_part * row_mean)
    input_local = (grads.astype(jnp.float32) + d_tokens).astype(jnp.bfloat16)
    states = (tokens.astype(jnp.float32) + attention).astype(jnp.bfloat16)
    gain_grad = jnp.sum(d_part * unit_part, axis=0).reshape(8, 128)
    gain_grad += swap(gain_grad, "pas", 1)
    gain_grad += swap(gain_grad, "pas", 2)

    def home(local):
        local = local.reshape(2, seq, 1024)
        back = local[1]
        over_x = swap(back, "pas", 2)
        over_core = swap(jnp.stack([back, over_x]), "pas", 1)

        def pick(host):
            way = host ^ me
            return jnp.where(way == 1, over_core[0], jnp.where(way == 2, over_x, over_core[1]))

        zero = jnp.zeros_like(back)
        return jnp.stack(
            [
                local[0],
                jnp.where(own_count >= 2, back, zero),
                jnp.where(own_count == 4, pick(host0), zero),
                jnp.where(own_count == 4, pick(host1), zero),
            ]
        )

    return home(states), home(input_local), gain_grad.reshape(1024)


def solution(mesh):
    placed = (
        P(("grp", "pas"), None, "fsdp"),
        P(("grp", "pas"), None, "fsdp"),
        P(("grp", "pas")),
        P(),
        P("pas", "fsdp"),
        P("pas", "fsdp"),
        P("pas", "fsdp"),
        P("fsdp", "pas"),
    )
    sizes = dict(mesh.shape)
    fast = sizes["grp"] == 2 and sizes["pas"] == 4 and sizes["fsdp"] == 4
    return jax.shard_map(
        fast_body if fast else general_body,
        mesh=mesh,
        in_specs=placed,
        out_specs=(
            P(("grp", "pas"), None, "fsdp"),
            P(("grp", "pas"), None, "fsdp"),
            P(("grp", "fsdp")),
        ),
        check_vma=False,
    )
```

```python
import jax
import jax.numpy as jnp
from jax import lax
from jax.experimental import pallas as pl
from jax.experimental.pallas import tpu as pltpu
from jax.sharding import PartitionSpec as P

HD = 64
BAL = 2
EPSILON = 1e-06
VMEM_LIMIT = 50 * 2**20


def entering(shard, axis, combine, identity):
    length, position = (lax.axis_size(axis), lax.axis_index(axis))
    everything = lax.all_gather(shard, axis)
    start = jnp.broadcast_to(jnp.asarray(identity, shard.dtype), shard.shape)

    def lap(k, before):
        reached = k < position
        new = combine(before, everything[k])
        return jnp.where(reached, new, before)

    return lax.fori_loop(0, length, lap, start)


def add_counts(earlier, later):
    return earlier + later


def general_body(passages, cotangent, passage_counts, norm_gain, w_query, w_key, w_value, w_out):
    peer_total = lax.axis_size("pas")
    slots, seq_len, part_width = passages.shape
    flat_width = seq_len * part_width
    own_count = passage_counts[0]
    first_rank = entering(passage_counts, "pas", add_counts, jnp.zeros_like(passage_counts))[0]
    slot_index = jnp.arange(slots, dtype=jnp.int32)
    slot_rank = first_rank + slot_index
    is_live = slot_index < own_count
    peer_index = jnp.arange(peer_total, dtype=jnp.int32)
    routing_mask = is_live[None, :] & ((slot_rank % peer_total)[None, :] == peer_index[:, None])
    routing = routing_mask.astype(jnp.bfloat16)
    sent_rank = jnp.max(jnp.where(routing_mask, slot_rank[None, :], -1), axis=1).astype(jnp.int32)
    send_tokens = jnp.dot(
        routing, passages.reshape(slots, flat_width), preferred_element_type=jnp.float32
    ).astype(jnp.bfloat16)
    send_grads = jnp.dot(
        routing, cotangent.reshape(slots, flat_width), preferred_element_type=jnp.float32
    ).astype(jnp.bfloat16)
    got_tokens, got_grads, got_rank = (
        lax.all_to_all(send_tokens, "pas", split_axis=0, concat_axis=0, tiled=True),
        lax.all_to_all(send_grads, "pas", split_axis=0, concat_axis=0, tiled=True),
        lax.all_to_all(sent_rank, "pas", split_axis=0, concat_axis=0, tiled=True),
    )
    picked_mask = (got_rank[None, :] >= 0) & (
        got_rank[None, :] // peer_total == jnp.arange(BAL, dtype=jnp.int32)[:, None]
    )
    picked = picked_mask.astype(jnp.bfloat16)
    returned = jnp.transpose(picked)
    local_tokens = (
        jnp.dot(picked, got_tokens, preferred_element_type=jnp.float32)
        .astype(jnp.bfloat16)
        .reshape(BAL, seq_len, part_width)
    )
    local_grads = (
        jnp.dot(picked, got_grads, preferred_element_type=jnp.float32)
        .astype(jnp.bfloat16)
        .reshape(BAL, seq_len, part_width)
    )
    query_w, key_w, value_w, out_w = (
        lax.all_gather(w_query, "pas", axis=0, tiled=True),
        lax.all_gather(w_key, "pas", axis=0, tiled=True),
        lax.all_gather(w_value, "pas", axis=0, tiled=True),
        lax.all_gather(w_out, "pas", axis=1, tiled=True),
    )
    full_tokens = lax.all_gather(local_tokens, "fsdp", axis=2, tiled=True)
    width = full_tokens.shape[2]
    feature_start = lax.axis_index("fsdp") * part_width
    full_f32 = full_tokens.astype(jnp.float32)
    inverse = lax.rsqrt(jnp.mean(full_f32 * full_f32, axis=-1, keepdims=True) + EPSILON)
    unit_rows = full_f32 * inverse
    normed = (unit_rows * norm_gain).astype(jnp.bfloat16)
    local_cols = query_w.shape[1]
    head_count = local_cols // HD
    flat_rows = normed.reshape(BAL * seq_len, width)

    def project(weight):
        result = jnp.dot(flat_rows, weight, preferred_element_type=jnp.float32).astype(jnp.bfloat16)
        return result.reshape(BAL, seq_len, head_count, HD)

    query = project(query_w)
    keys = project(key_w)
    values = project(value_w)
    scores = jnp.einsum("blhe,bmhe->bhlm", query, keys, preferred_element_type=jnp.float32)
    probs = jax.nn.softmax(scores, axis=-1)
    probs_low = probs.astype(jnp.bfloat16)
    context = jnp.einsum(
        "bhlm,bmhe->blhe", probs_low, values, preferred_element_type=jnp.float32
    ).astype(jnp.bfloat16)
    context_rows = context.reshape(BAL * seq_len, local_cols)
    partial_out = jnp.dot(context_rows, out_w, preferred_element_type=jnp.float32).reshape(
        BAL, seq_len, width
    )
    attention = lax.psum_scatter(
        partial_out.astype(jnp.bfloat16), "fsdp", scatter_dimension=2, tiled=True
    ).astype(jnp.float32)
    states = (local_tokens.astype(jnp.float32) + attention).astype(jnp.bfloat16)
    states_back = jnp.dot(
        returned, states.reshape(BAL, flat_width), preferred_element_type=jnp.float32
    ).astype(jnp.bfloat16)
    states_home = lax.all_to_all(states_back, "pas", split_axis=0, concat_axis=0, tiled=True)
    upstream_rows = lax.all_gather(local_grads, "fsdp", axis=2, tiled=True).reshape(
        BAL * seq_len, width
    )
    d_context = jnp.einsum(
        "td,cd->tc", upstream_rows, out_w, preferred_element_type=jnp.float32
    ).astype(jnp.bfloat16)
    d_context = d_context.reshape(BAL, seq_len, head_count, HD)
    d_values = jnp.einsum(
        "bhlm,blhe->bmhe", probs_low, d_context, preferred_element_type=jnp.float32
    ).astype(jnp.bfloat16)
    d_probs = jnp.einsum("blhe,bmhe->bhlm", d_context, values, preferred_element_type=jnp.float32)
    d_scores = (probs * (d_probs - jnp.sum(d_probs * probs, axis=-1, keepdims=True))).astype(
        jnp.bfloat16
    )
    d_query = jnp.einsum(
        "bhlm,bmhe->blhe", d_scores, keys, preferred_element_type=jnp.float32
    ).astype(jnp.bfloat16)
    d_keys = jnp.einsum(
        "bhlm,blhe->bmhe", d_scores, query, preferred_element_type=jnp.float32
    ).astype(jnp.bfloat16)

    def back_project(grad, weight):
        grad_rows = grad.reshape(BAL * seq_len, local_cols)
        return jnp.einsum("tc,dc->td", grad_rows, weight, preferred_element_type=jnp.float32)

    d_normed = (
        back_project(d_query, query_w)
        + back_project(d_keys, key_w)
        + back_project(d_values, value_w)
    )
    d_normed_part = lax.psum_scatter(
        d_normed.reshape(BAL, seq_len, width).astype(jnp.bfloat16),
        "fsdp",
        scatter_dimension=2,
        tiled=True,
    ).astype(jnp.float32)
    unit_part = lax.dynamic_slice_in_dim(unit_rows, feature_start, part_width, 2)
    gain_part = lax.dynamic_slice_in_dim(norm_gain, feature_start, part_width, 0)
    d_unit = d_normed_part * gain_part
    row_total = lax.psum(jnp.sum(d_unit * unit_part, axis=-1, keepdims=True), "fsdp")
    row_mean = row_total / width
    d_tokens = inverse * (d_unit - unit_part * row_mean)
    grads_local = (local_grads.astype(jnp.float32) + d_tokens).astype(jnp.bfloat16)
    gain_grad = lax.psum(jnp.sum(d_normed_part * unit_part, axis=(0, 1)), "pas")
    grads_back = jnp.dot(
        returned, grads_local.reshape(BAL, flat_width), preferred_element_type=jnp.float32
    ).astype(jnp.bfloat16)
    grads_home = lax.all_to_all(grads_back, "pas", split_axis=0, concat_axis=0, tiled=True)
    routing_back = jnp.transpose(routing)
    encoded = (
        jnp.dot(routing_back, states_home, preferred_element_type=jnp.float32)
        .astype(jnp.bfloat16)
        .reshape(slots, seq_len, part_width)
    )
    input_grad = (
        jnp.dot(routing_back, grads_home, preferred_element_type=jnp.float32)
        .astype(jnp.bfloat16)
        .reshape(slots, seq_len, part_width)
    )
    return (encoded, input_grad, gain_grad)


def swap(array, axis, bit):
    return lax.ppermute(array, axis, [(i, i ^ bit) for i in range(lax.axis_size(axis))])


def dot_nn(a, b):
    return jnp.dot(a, b, preferred_element_type=jnp.float32)


def dot_nt(a, b):
    return lax.dot_general(a, b, (((1,), (1,)), ((), ())), preferred_element_type=jnp.float32)


def dot_tn(a, b):
    return lax.dot_general(a, b, (((0,), (0,)), ((), ())), preferred_element_type=jnp.float32)


def stream(weights, pos, held, sems):
    started = {}
    for i in range(4):
        for w, pieces in enumerate(weights):
            piece = pieces[i]
            if isinstance(piece, list):
                parts = []
                for j, chunk in enumerate(piece):
                    size = chunk.shape[0]
                    at = pl.multiple_of((j ^ (2 * pos[1])) * size, size)
                    parts.append((chunk, held.at[w, i, pl.ds(at, size)], sems.at[w, i, j]))
            else:
                parts = [(piece, held.at[w, i], sems.at[w, i, 0])]
            started[w, i] = [pltpu.make_async_copy(*part) for part in parts]
            for copy in started[w, i]:
                copy.start()

    def ready(w, i):
        for copy in started[w, i]:
            copy.wait()
        return held[w, i]

    return ready


def project_kernel(weights, pos, dense, out, held, sems):
    ready = stream(weights, pos, held, sems)
    total = 0.0
    for i in range(4):
        total += dot_nn(dense[0][pos[0] ^ i], ready(0, i))
    out[...] = total.astype(out.dtype)


def project_out_kernel(weights, pos, dense, out, held, sems):
    ready = stream(weights, pos, held, sems)
    total = 0.0
    for i in range(4):
        total += dot_nt(dense[0][pos[0] ^ i], ready(0, i))
    out[...] = total.astype(out.dtype)


def emit_kernel(weights, pos, dense, out, held, sems):
    ready = stream(weights, pos, held, sems)
    rows = dense[0][...]
    for i in range(4):
        out[pos[0] ^ i] = dot_nn(rows, ready(0, i)).astype(out.dtype)


def back_kernel(weights, pos, dense, out, held, sems):
    ready = stream(weights, pos, held, sems)
    grads = [d[...] for d in dense]
    for i in range(4):
        total = sum(dot_nt(g, ready(w, i)) for w, g in enumerate(grads))
        out[pos[0] ^ i] = total.astype(out.dtype)


def call(kernel, pos, dense, weights, out_shape):
    flat, tree = jax.tree.flatten(weights)
    count = len(weights)

    def run(pos_ref, *refs):
        dense_refs = refs[: len(dense)]
        weight_refs = jax.tree.unflatten(tree, refs[len(dense) : len(dense) + len(flat)])
        out, held, sems = refs[len(dense) + len(flat) :]
        kernel(weight_refs, pos_ref, dense_refs, out, held, sems)

    size = count * 2**22
    return pl.pallas_call(
        run,
        in_specs=[pl.BlockSpec(memory_space=pltpu.SMEM)]
        + [pl.BlockSpec(memory_space=pltpu.VMEM)] * len(dense)
        + [pl.BlockSpec(memory_space=pl.ANY)] * len(flat),
        out_specs=pl.BlockSpec(memory_space=pltpu.VMEM),
        out_shape=out_shape,
        scratch_shapes=[
            pltpu.VMEM((count, 4, 1024, 1024), jnp.bfloat16),
            pltpu.SemaphoreType.DMA((count, 4, 4)),
        ],
        cost_estimate=pl.CostEstimate(flops=512 * size, bytes_accessed=2 * size, transcendentals=0),
        compiler_params=pltpu.CompilerParams(vmem_limit_bytes=VMEM_LIMIT),
    )(pos, *dense, *flat)


def head_pairs(width):
    return [pl.ds(pair * 128, 128) for pair in range(width // 128)]


def first_head(seq):
    return lax.broadcasted_iota(jnp.int32, (seq, 128), 1) < HD


def split_heads(array):
    first = first_head(array.shape[0])
    mask0 = jnp.where(first, 1.0, 0.0).astype(array.dtype)
    mask1 = jnp.where(first, 0.0, 1.0).astype(array.dtype)
    return jnp.concatenate([array * mask0, array * mask1], axis=0)


def join_heads(both):
    seq = both.shape[0] // 2
    return jnp.where(first_head(seq), both[:seq], both[seq:])


def softmax_pair(scores):
    seq = scores.shape[0]
    probs = []
    for h in range(2):
        s = scores[:, h * seq : (h + 1) * seq]
        e = jnp.exp(s - jnp.max(s, axis=-1, keepdims=True))
        probs.append(e / jnp.sum(e, axis=-1, keepdims=True))
    return probs


def attention_kernel(q_ref, k_ref, v_ref, ctx_ref):
    for at in head_pairs(q_ref.shape[1]):
        probs = softmax_pair(dot_nt(q_ref[:, at], split_heads(k_ref[:, at])))
        low = jnp.concatenate([p.astype(jnp.bfloat16) for p in probs], axis=1)
        ctx_ref[:, at] = dot_nn(low, split_heads(v_ref[:, at])).astype(jnp.bfloat16)


def attention_back_kernel(q_ref, k_ref, v_ref, dc_ref, dq_ref, dk_ref, dv_ref):
    seq = q_ref.shape[0]
    for at in head_pairs(q_ref.shape[1]):
        q, dc = q_ref[:, at], dc_ref[:, at]
        keys = split_heads(k_ref[:, at])
        probs = softmax_pair(dot_nt(q, keys))
        d_probs = dot_nt(dc, split_heads(v_ref[:, at]))
        d_scores = []
        for h in range(2):
            dp = d_probs[:, h * seq : (h + 1) * seq]
            ds = probs[h] * (dp - jnp.sum(dp * probs[h], axis=-1, keepdims=True))
            d_scores.append(ds.astype(jnp.bfloat16))
        low = jnp.concatenate([p.astype(jnp.bfloat16) for p in probs], axis=1)
        ds = jnp.concatenate(d_scores, axis=1)
        dq_ref[:, at] = dot_nn(ds, keys).astype(jnp.bfloat16)
        dv_ref[:, at] = join_heads(dot_tn(low, dc)).astype(jnp.bfloat16)
        dk_ref[:, at] = join_heads(dot_tn(ds, q)).astype(jnp.bfloat16)


def attend(kernel, arrays, outputs):
    rows, cols = arrays[0].shape
    spec = pl.BlockSpec((rows // BAL, cols // 2), lambda i, j: (i, j))
    shape = jax.ShapeDtypeStruct((rows, cols), jnp.bfloat16)
    many = len(arrays) + outputs
    return pl.pallas_call(
        kernel,
        grid=(BAL, 2),
        in_specs=[spec] * len(arrays),
        out_specs=[spec] * outputs,
        out_shape=[shape] * outputs,
        cost_estimate=pl.CostEstimate(
            flops=32 * 8 * 128 * 128 * 128, bytes_accessed=many * 2 * rows * cols, transcendentals=2**19
        ),
        compiler_params=pltpu.CompilerParams(vmem_limit_bytes=VMEM_LIMIT),
    )(*arrays)


ANYWHERE = pl.BlockSpec(memory_space=pl.ANY)


def cut(weight, block, earlier):
    def copy(block_ref, rows, *refs):
        refs[-1][...] = rows[...]

    return pl.pallas_call(
        copy,
        grid_spec=pltpu.PrefetchScalarGridSpec(
            num_scalar_prefetch=1,
            grid=(1,),
            in_specs=[pl.BlockSpec((256, 1024), lambda i, block: (block[0], 0))]
            + [ANYWHERE] * len(earlier),
            out_specs=pl.BlockSpec((256, 1024), lambda i, block: (0, 0)),
        ),
        out_shape=jax.ShapeDtypeStruct((256, 1024), weight.dtype),
        cost_estimate=pl.CostEstimate(flops=0, bytes_accessed=2**20, transcendentals=0),
    )(block.reshape(1), weight, *earlier)


def after(array, *earlier):
    def nothing(*refs):
        pass

    return pl.pallas_call(
        nothing,
        in_specs=[ANYWHERE] * (1 + len(earlier)),
        out_specs=ANYWHERE,
        out_shape=jax.ShapeDtypeStruct(array.shape, array.dtype),
        input_output_aliases={0: 0},
    )(array, *earlier)


def far_block(chunks, group):
    low, high = jnp.concatenate(chunks[:2]), jnp.concatenate(chunks[2:])
    return jnp.where(group == 0, jnp.concatenate([low, high]), jnp.concatenate([high, low]))


def fast_body(passages, cotangent, passage_counts, norm_gain, w_query, w_key, w_value, w_out):
    me = lax.axis_index("pas")
    group = lax.axis_index("grp")
    feature = lax.axis_index("fsdp")
    seq = passages.shape[1]
    pos = jnp.stack([me, group]).astype(jnp.int32)

    counts = lax.all_gather(passage_counts, "pas", axis=0, tiled=True)
    index = jnp.arange(4, dtype=jnp.int32)
    single = counts == 1
    source = jnp.sum(jnp.where(counts == 4, index, 0))
    rank = lambda d: jnp.minimum(jnp.sum((single & (index < d)).astype(jnp.int32)), 1)
    host0 = jnp.min(jnp.where(single, index, 4))
    host1 = jnp.max(jnp.where(single, index, -1))
    own_count = passage_counts[0]
    relation = me ^ source

    def send_second(array):
        extra = array[2:4]
        extra_core = swap(extra, "pas", 1)
        there = rank(me ^ 2)
        picked = jnp.where(source == me, extra, extra_core)
        return extra_core, jnp.where(there == 0, picked[0], picked[1])

    def second(array, extra_core, got_x):
        from_core = jnp.where(rank(me) == 0, extra_core[0], extra_core[1])
        foreign = jnp.where(relation == 1, from_core, got_x)
        return jnp.where(own_count >= 2, array[1], foreign)

    weights = (w_key, w_query, w_value, w_out)
    over_x, over_y = [], []

    def send(*earlier):
        i = len(over_x)
        chunk = cut(weights[i // 2], group * 2 + i % 2, earlier)
        over_x.append(swap(chunk, "pas", 2))

    def forward():
        over_y.append(swap(over_x[len(over_y)], "grp", 1))

    def fetch(i):
        far = far_block(over_x[i : i + 2] + over_y[i : i + 2], group)
        return [weights[i // 2], swap(weights[i // 2], "pas", 1), far, swap(far, "pas", 1)]

    send()
    tokens_core, tokens_sent = send_second(passages)
    grads_core, grads_sent = send_second(cotangent)
    tokens_x = swap(tokens_sent, "pas", 2)
    grads_x = swap(grads_sent, "pas", 2)
    tokens = jnp.concatenate([passages[0], second(passages, tokens_core, tokens_x)], axis=0)
    grads = jnp.concatenate([cotangent[0], second(cotangent, grads_core, grads_x)], axis=0)
    all_tokens = lax.all_gather(tokens, "fsdp", axis=0)
    all_grads = lax.all_gather(grads, "fsdp", axis=0)

    tokens_f32 = all_tokens.astype(jnp.float32)
    width = norm_gain.shape[0]
    gain = norm_gain.reshape(4, 1, 1024)
    inverse = lax.rsqrt(
        jnp.sum(tokens_f32 * tokens_f32, axis=(0, 2), keepdims=True) / width + EPSILON
    )
    normed = (tokens_f32 * inverse * gain).astype(jnp.bfloat16)

    rows_shape = jax.ShapeDtypeStruct((2 * seq, 1024), jnp.bfloat16)
    wide_shape = jax.ShapeDtypeStruct((4, 2 * seq, 1024), jnp.bfloat16)

    def project(w):
        return call(project_kernel, pos, [normed], [w], rows_shape)

    send(tokens_sent, grads_sent)
    forward()
    send(over_x[0], tokens_x, grads_x)
    forward()
    send(over_x[1], over_y[0], grads)
    key_w = fetch(0)
    forward()
    send(over_x[2], over_y[1])
    forward()
    send(over_x[3], over_y[2])
    query_w = fetch(2)
    forward()
    keys = project(key_w)
    send(over_x[4], over_y[3], keys)
    forward()
    query = project(query_w)
    send(over_x[5], over_y[4], query)
    value_w = fetch(4)
    forward()
    forward()
    far = over_x[6:] + over_y[6:]
    out_w = [w_out, swap(w_out, "pas", 1), far, [swap(c, "pas", 1) for c in far]]
    values = project(value_w)
    (context,) = attend(attention_kernel, (query, keys, values), 1)
    partial_out = call(emit_kernel, pos, [context], [out_w], wide_shape)
    attention = lax.psum_scatter(partial_out, "fsdp", scatter_dimension=0)
    d_context = call(project_out_kernel, pos, [after(all_grads, partial_out)], [out_w], rows_shape)
    d_query, d_keys, d_values = attend(attention_back_kernel, (query, keys, values, d_context), 3)
    d_normed = call(
        back_kernel, pos, [d_query, d_keys, d_values], [query_w, key_w, value_w], wide_shape
    )

    d_normed = after(d_normed, attention)
    d_part = lax.psum_scatter(d_normed, "fsdp", scatter_dimension=0).astype(jnp.float32)

    row_total = jnp.sum(
        d_normed.astype(jnp.float32) * gain * (tokens_f32 * inverse), axis=(0, 2)
    ).reshape(2, seq)
    row_total += swap(row_total, "fsdp", 1)
    row_total += swap(row_total, "fsdp", 2)
    row_mean = row_total.reshape(2 * seq, 1) / width

    gain_part = lax.dynamic_slice_in_dim(norm_gain, feature * 1024, 1024, 0)
    inverse_rows = inverse.reshape(2 * seq, 1)
    unit_part = tokens.astype(jnp.float32) * inverse_rows
    d_tokens = inverse_rows * (d_part * gain_part - unit_part * row_mean)
    input_local = (grads.astype(jnp.float32) + d_tokens).astype(jnp.bfloat16)
    states = (tokens.astype(jnp.float32) + attention.astype(jnp.float32)).astype(jnp.bfloat16)
    gain_grad = jnp.sum(d_part * unit_part, axis=0).reshape(8, 128)
    gain_grad += swap(gain_grad, "pas", 1)
    gain_grad += swap(gain_grad, "pas", 2)

    def home(local):
        local = local.reshape(2, seq, 1024)
        back = local[1]
        over_x = swap(back, "pas", 2)
        over_core = swap(jnp.stack([back, over_x]), "pas", 1)

        def pick(host):
            way = host ^ me
            return jnp.where(way == 1, over_core[0], jnp.where(way == 2, over_x, over_core[1]))

        zero = jnp.zeros_like(back)
        return jnp.stack(
            [
                local[0],
                jnp.where(own_count >= 2, back, zero),
                jnp.where(own_count == 4, pick(host0), zero),
                jnp.where(own_count == 4, pick(host1), zero),
            ]
        )

    return home(states), home(input_local), gain_grad.reshape(1024)


def solution(mesh):
    placed = (
        P(("grp", "pas"), None, "fsdp"),
        P(("grp", "pas"), None, "fsdp"),
        P(("grp", "pas")),
        P(),
        P("pas", "fsdp"),
        P("pas", "fsdp"),
        P("pas", "fsdp"),
        P("fsdp", "pas"),
    )
    sizes = dict(mesh.shape)
    fast = sizes["grp"] == 2 and sizes["pas"] == 4 and sizes["fsdp"] == 4
    return jax.shard_map(
        fast_body if fast else general_body,
        mesh=mesh,
        in_specs=placed,
        out_specs=(
            P(("grp", "pas"), None, "fsdp"),
            P(("grp", "pas"), None, "fsdp"),
            P(("grp", "fsdp")),
        ),
        check_vma=False,
    )
```

```python
import jax
import jax.numpy as jnp
from jax import lax
from jax.experimental import pallas as pl
from jax.experimental.pallas import tpu as pltpu
from jax.sharding import PartitionSpec as P

HD = 64
BAL = 2
EPSILON = 1e-06
VMEM_LIMIT = 50 * 2**20


def entering(shard, axis, combine, identity):
    length, position = (lax.axis_size(axis), lax.axis_index(axis))
    everything = lax.all_gather(shard, axis)
    start = jnp.broadcast_to(jnp.asarray(identity, shard.dtype), shard.shape)

    def lap(k, before):
        reached = k < position
        new = combine(before, everything[k])
        return jnp.where(reached, new, before)

    return lax.fori_loop(0, length, lap, start)


def add_counts(earlier, later):
    return earlier + later


def general_body(passages, cotangent, passage_counts, norm_gain, w_query, w_key, w_value, w_out):
    peer_total = lax.axis_size("pas")
    slots, seq_len, part_width = passages.shape
    flat_width = seq_len * part_width
    own_count = passage_counts[0]
    first_rank = entering(passage_counts, "pas", add_counts, jnp.zeros_like(passage_counts))[0]
    slot_index = jnp.arange(slots, dtype=jnp.int32)
    slot_rank = first_rank + slot_index
    is_live = slot_index < own_count
    peer_index = jnp.arange(peer_total, dtype=jnp.int32)
    routing_mask = is_live[None, :] & ((slot_rank % peer_total)[None, :] == peer_index[:, None])
    routing = routing_mask.astype(jnp.bfloat16)
    sent_rank = jnp.max(jnp.where(routing_mask, slot_rank[None, :], -1), axis=1).astype(jnp.int32)
    send_tokens = jnp.dot(
        routing, passages.reshape(slots, flat_width), preferred_element_type=jnp.float32
    ).astype(jnp.bfloat16)
    send_grads = jnp.dot(
        routing, cotangent.reshape(slots, flat_width), preferred_element_type=jnp.float32
    ).astype(jnp.bfloat16)
    got_tokens, got_grads, got_rank = (
        lax.all_to_all(send_tokens, "pas", split_axis=0, concat_axis=0, tiled=True),
        lax.all_to_all(send_grads, "pas", split_axis=0, concat_axis=0, tiled=True),
        lax.all_to_all(sent_rank, "pas", split_axis=0, concat_axis=0, tiled=True),
    )
    picked_mask = (got_rank[None, :] >= 0) & (
        got_rank[None, :] // peer_total == jnp.arange(BAL, dtype=jnp.int32)[:, None]
    )
    picked = picked_mask.astype(jnp.bfloat16)
    returned = jnp.transpose(picked)
    local_tokens = (
        jnp.dot(picked, got_tokens, preferred_element_type=jnp.float32)
        .astype(jnp.bfloat16)
        .reshape(BAL, seq_len, part_width)
    )
    local_grads = (
        jnp.dot(picked, got_grads, preferred_element_type=jnp.float32)
        .astype(jnp.bfloat16)
        .reshape(BAL, seq_len, part_width)
    )
    query_w, key_w, value_w, out_w = (
        lax.all_gather(w_query, "pas", axis=0, tiled=True),
        lax.all_gather(w_key, "pas", axis=0, tiled=True),
        lax.all_gather(w_value, "pas", axis=0, tiled=True),
        lax.all_gather(w_out, "pas", axis=1, tiled=True),
    )
    full_tokens = lax.all_gather(local_tokens, "fsdp", axis=2, tiled=True)
    width = full_tokens.shape[2]
    feature_start = lax.axis_index("fsdp") * part_width
    full_f32 = full_tokens.astype(jnp.float32)
    inverse = lax.rsqrt(jnp.mean(full_f32 * full_f32, axis=-1, keepdims=True) + EPSILON)
    unit_rows = full_f32 * inverse
    normed = (unit_rows * norm_gain).astype(jnp.bfloat16)
    local_cols = query_w.shape[1]
    head_count = local_cols // HD
    flat_rows = normed.reshape(BAL * seq_len, width)

    def project(weight):
        result = jnp.dot(flat_rows, weight, preferred_element_type=jnp.float32).astype(jnp.bfloat16)
        return result.reshape(BAL, seq_len, head_count, HD)

    query = project(query_w)
    keys = project(key_w)
    values = project(value_w)
    scores = jnp.einsum("blhe,bmhe->bhlm", query, keys, preferred_element_type=jnp.float32)
    probs = jax.nn.softmax(scores, axis=-1)
    probs_low = probs.astype(jnp.bfloat16)
    context = jnp.einsum(
        "bhlm,bmhe->blhe", probs_low, values, preferred_element_type=jnp.float32
    ).astype(jnp.bfloat16)
    context_rows = context.reshape(BAL * seq_len, local_cols)
    partial_out = jnp.dot(context_rows, out_w, preferred_element_type=jnp.float32).reshape(
        BAL, seq_len, width
    )
    attention = lax.psum_scatter(
        partial_out.astype(jnp.bfloat16), "fsdp", scatter_dimension=2, tiled=True
    ).astype(jnp.float32)
    states = (local_tokens.astype(jnp.float32) + attention).astype(jnp.bfloat16)
    states_back = jnp.dot(
        returned, states.reshape(BAL, flat_width), preferred_element_type=jnp.float32
    ).astype(jnp.bfloat16)
    states_home = lax.all_to_all(states_back, "pas", split_axis=0, concat_axis=0, tiled=True)
    upstream_rows = lax.all_gather(local_grads, "fsdp", axis=2, tiled=True).reshape(
        BAL * seq_len, width
    )
    d_context = jnp.einsum(
        "td,cd->tc", upstream_rows, out_w, preferred_element_type=jnp.float32
    ).astype(jnp.bfloat16)
    d_context = d_context.reshape(BAL, seq_len, head_count, HD)
    d_values = jnp.einsum(
        "bhlm,blhe->bmhe", probs_low, d_context, preferred_element_type=jnp.float32
    ).astype(jnp.bfloat16)
    d_probs = jnp.einsum("blhe,bmhe->bhlm", d_context, values, preferred_element_type=jnp.float32)
    d_scores = (probs * (d_probs - jnp.sum(d_probs * probs, axis=-1, keepdims=True))).astype(
        jnp.bfloat16
    )
    d_query = jnp.einsum(
        "bhlm,bmhe->blhe", d_scores, keys, preferred_element_type=jnp.float32
    ).astype(jnp.bfloat16)
    d_keys = jnp.einsum(
        "bhlm,blhe->bmhe", d_scores, query, preferred_element_type=jnp.float32
    ).astype(jnp.bfloat16)

    def back_project(grad, weight):
        grad_rows = grad.reshape(BAL * seq_len, local_cols)
        return jnp.einsum("tc,dc->td", grad_rows, weight, preferred_element_type=jnp.float32)

    d_normed = (
        back_project(d_query, query_w)
        + back_project(d_keys, key_w)
        + back_project(d_values, value_w)
    )
    d_normed_part = lax.psum_scatter(
        d_normed.reshape(BAL, seq_len, width).astype(jnp.bfloat16),
        "fsdp",
        scatter_dimension=2,
        tiled=True,
    ).astype(jnp.float32)
    unit_part = lax.dynamic_slice_in_dim(unit_rows, feature_start, part_width, 2)
    gain_part = lax.dynamic_slice_in_dim(norm_gain, feature_start, part_width, 0)
    d_unit = d_normed_part * gain_part
    row_total = lax.psum(jnp.sum(d_unit * unit_part, axis=-1, keepdims=True), "fsdp")
    row_mean = row_total / width
    d_tokens = inverse * (d_unit - unit_part * row_mean)
    grads_local = (local_grads.astype(jnp.float32) + d_tokens).astype(jnp.bfloat16)
    gain_grad = lax.psum(jnp.sum(d_normed_part * unit_part, axis=(0, 1)), "pas")
    grads_back = jnp.dot(
        returned, grads_local.reshape(BAL, flat_width), preferred_element_type=jnp.float32
    ).astype(jnp.bfloat16)
    grads_home = lax.all_to_all(grads_back, "pas", split_axis=0, concat_axis=0, tiled=True)
    routing_back = jnp.transpose(routing)
    encoded = (
        jnp.dot(routing_back, states_home, preferred_element_type=jnp.float32)
        .astype(jnp.bfloat16)
        .reshape(slots, seq_len, part_width)
    )
    input_grad = (
        jnp.dot(routing_back, grads_home, preferred_element_type=jnp.float32)
        .astype(jnp.bfloat16)
        .reshape(slots, seq_len, part_width)
    )
    return (encoded, input_grad, gain_grad)


ANYWHERE = pl.BlockSpec(memory_space=pl.ANY)


def swap(array, axis, bit):
    return lax.ppermute(array, axis, [(i, i ^ bit) for i in range(lax.axis_size(axis))])


def dot_nn(a, b):
    return jnp.dot(a, b, preferred_element_type=jnp.float32)


def dot_nt(a, b):
    return lax.dot_general(a, b, (((1,), (1,)), ((), ())), preferred_element_type=jnp.float32)


def dot_tn(a, b):
    return lax.dot_general(a, b, (((0,), (0,)), ((), ())), preferred_element_type=jnp.float32)


def places(group, count):
    first, second = group * 512, (1 - group) * 512
    if count == 4:
        rows = [first, first + 256, second, second + 256]
    else:
        rows = [first, first + 256, 384, second, second + 256, 896]
    return [pl.multiple_of(r, 128) for r in rows]


def stream(weights, pos, held, sems):
    started = {}
    for i in range(4):
        for w, pieces in enumerate(weights):
            piece = pieces[i]
            if isinstance(piece, list):
                parts = []
                for j, (chunk, at) in enumerate(zip(piece, places(pos[1], len(piece)))):
                    size = 128 if len(piece) == 6 and j % 3 else 256
                    source = chunk
                    if j == 5:
                        source = chunk.at[pl.ds(128, 128)]
                    elif len(piece) == 6 and j == 2:
                        source = chunk.at[pl.ds(0, 128)]
                    parts.append((source, held.at[w, i, pl.ds(at, size)], sems.at[w, i, j]))
            else:
                parts = [(piece, held.at[w, i], sems.at[w, i, 0])]
            started[w, i] = [pltpu.make_async_copy(*part) for part in parts]
            for copy in started[w, i]:
                copy.start()

    def ready(w, i):
        for copy in started[w, i]:
            copy.wait()
        return held[w, i]

    return ready


def project_kernel(weights, pos, dense, out, held, sems):
    ready = stream(weights, pos, held, sems)
    total = 0.0
    for i in range(4):
        total += dot_nn(dense[0][pos[0] ^ i], ready(0, i))
    out[...] = total.astype(out.dtype)


def project_out_kernel(weights, pos, dense, out, held, sems):
    ready = stream(weights, pos, held, sems)
    total = 0.0
    for i in range(4):
        total += dot_nt(dense[0][pos[0] ^ i], ready(0, i))
    out[...] = total.astype(out.dtype)


def emit_kernel(weights, pos, dense, out, held, sems):
    ready = stream(weights, pos, held, sems)
    rows = dense[0][...]
    for i in range(4):
        out[pos[0] ^ i] = dot_nn(rows, ready(0, i)).astype(out.dtype)


def back_kernel(weights, pos, dense, out, held, sems):
    ready = stream(weights, pos, held, sems)
    grads = [d[...] for d in dense]
    for i in range(4):
        total = sum(dot_nt(g, ready(w, i)) for w, g in enumerate(grads))
        out[pos[0] ^ i] = total.astype(out.dtype)


def call(kernel, pos, dense, weights, out_shape, *earlier):
    flat, tree = jax.tree.flatten(weights)
    count = len(weights)

    def run(pos_ref, *refs):
        dense_refs = refs[: len(dense)]
        weight_refs = jax.tree.unflatten(tree, refs[len(dense) : len(dense) + len(flat)])
        out, held, sems = refs[-3:]
        kernel(weight_refs, pos_ref, dense_refs, out, held, sems)

    size = count * 2**22
    return pl.pallas_call(
        run,
        in_specs=[pl.BlockSpec(memory_space=pltpu.SMEM)]
        + [pl.BlockSpec(memory_space=pltpu.VMEM)] * len(dense)
        + [ANYWHERE] * (len(flat) + len(earlier)),
        out_specs=pl.BlockSpec(memory_space=pltpu.VMEM),
        out_shape=out_shape,
        scratch_shapes=[
            pltpu.VMEM((count, 4, 1024, 1024), jnp.bfloat16),
            pltpu.SemaphoreType.DMA((count, 4, 6)),
        ],
        cost_estimate=pl.CostEstimate(flops=512 * size, bytes_accessed=2 * size, transcendentals=0),
        compiler_params=pltpu.CompilerParams(vmem_limit_bytes=VMEM_LIMIT),
    )(pos, *dense, *flat, *earlier)


def head_pairs(width):
    return [pl.ds(pair * 128, 128) for pair in range(width // 128)]


def first_head(seq):
    return lax.broadcasted_iota(jnp.int32, (seq, 128), 1) < HD


def split_heads(array):
    first = first_head(array.shape[0])
    mask0 = jnp.where(first, 1.0, 0.0).astype(array.dtype)
    mask1 = jnp.where(first, 0.0, 1.0).astype(array.dtype)
    return jnp.concatenate([array * mask0, array * mask1], axis=0)


def join_heads(both):
    seq = both.shape[0] // 2
    return jnp.where(first_head(seq), both[:seq], both[seq:])


def softmax_pair(scores):
    seq = scores.shape[0]
    probs = []
    for h in range(2):
        s = scores[:, h * seq : (h + 1) * seq]
        e = jnp.exp(s - jnp.max(s, axis=-1, keepdims=True))
        probs.append(e / jnp.sum(e, axis=-1, keepdims=True))
    return probs


def attention_kernel(q_ref, k_ref, v_ref, ctx_ref):
    for at in head_pairs(q_ref.shape[1]):
        probs = softmax_pair(dot_nt(q_ref[:, at], split_heads(k_ref[:, at])))
        low = jnp.concatenate([p.astype(jnp.bfloat16) for p in probs], axis=1)
        ctx_ref[:, at] = dot_nn(low, split_heads(v_ref[:, at])).astype(jnp.bfloat16)


def attention_back_kernel(q_ref, k_ref, v_ref, dc_ref, dq_ref, dk_ref, dv_ref):
    seq = q_ref.shape[0]
    for at in head_pairs(q_ref.shape[1]):
        q, dc = q_ref[:, at], dc_ref[:, at]
        keys = split_heads(k_ref[:, at])
        probs = softmax_pair(dot_nt(q, keys))
        d_probs = dot_nt(dc, split_heads(v_ref[:, at]))
        d_scores = []
        for h in range(2):
            dp = d_probs[:, h * seq : (h + 1) * seq]
            ds = probs[h] * (dp - jnp.sum(dp * probs[h], axis=-1, keepdims=True))
            d_scores.append(ds.astype(jnp.bfloat16))
        low = jnp.concatenate([p.astype(jnp.bfloat16) for p in probs], axis=1)
        ds = jnp.concatenate(d_scores, axis=1)
        dq_ref[:, at] = dot_nn(ds, keys).astype(jnp.bfloat16)
        dv_ref[:, at] = join_heads(dot_tn(low, dc)).astype(jnp.bfloat16)
        dk_ref[:, at] = join_heads(dot_tn(ds, q)).astype(jnp.bfloat16)


def attend(kernel, arrays, outputs):
    rows, cols = arrays[0].shape
    spec = pl.BlockSpec((rows // BAL, cols // 2), lambda i, j: (i, j))
    shape = jax.ShapeDtypeStruct((rows, cols), jnp.bfloat16)
    many = len(arrays) + outputs
    return pl.pallas_call(
        kernel,
        grid=(BAL, 2),
        in_specs=[spec] * len(arrays),
        out_specs=[spec] * outputs,
        out_shape=[shape] * outputs,
        cost_estimate=pl.CostEstimate(
            flops=32 * 8 * 128 * 128 * 128, bytes_accessed=many * 2 * rows * cols, transcendentals=2**19
        ),
        compiler_params=pltpu.CompilerParams(vmem_limit_bytes=VMEM_LIMIT),
    )(*arrays)


def cut(weight, block, rows, earlier):
    def copy(block_ref, source, *refs):
        refs[-1][...] = source[...]

    return pl.pallas_call(
        copy,
        grid_spec=pltpu.PrefetchScalarGridSpec(
            num_scalar_prefetch=1,
            grid=(1,),
            in_specs=[pl.BlockSpec((rows, 1024), lambda i, block: (block[0], 0))]
            + [ANYWHERE] * len(earlier),
            out_specs=pl.BlockSpec((rows, 1024), lambda i, block: (0, 0)),
        ),
        out_shape=jax.ShapeDtypeStruct((rows, 1024), weight.dtype),
        cost_estimate=pl.CostEstimate(flops=0, bytes_accessed=4096 * rows, transcendentals=0),
    )(block.reshape(1), weight, *earlier)


def cut_ends(weight, earlier):
    def copy(low, high, *refs):
        refs[-1][0:128] = low[...]
        refs[-1][128:256] = high[...]

    return pl.pallas_call(
        copy,
        grid=(1,),
        in_specs=[
            pl.BlockSpec((128, 1024), lambda i: (3, 0)),
            pl.BlockSpec((128, 1024), lambda i: (7, 0)),
        ]
        + [ANYWHERE] * len(earlier),
        out_specs=pl.BlockSpec((256, 1024), lambda i: (0, 0)),
        out_shape=jax.ShapeDtypeStruct((256, 1024), weight.dtype),
        cost_estimate=pl.CostEstimate(flops=0, bytes_accessed=2**20, transcendentals=0),
    )(weight, weight, *earlier)


def finish(d_part, tokens, grads, inverse, row_mean, gain, *earlier):
    def kernel(d_ref, x_ref, g_ref, inverse_ref, mean_ref, gain_ref, *refs):
        grad_out, gain_out = refs[-2:]
        d = d_ref[...].astype(jnp.float32)
        scale = inverse_ref[...]
        unit = x_ref[...].astype(jnp.float32) * scale
        d_tokens = scale * (d * gain_ref[...] - unit * mean_ref[...])
        grad_out[...] = (g_ref[...].astype(jnp.float32) + d_tokens).astype(grad_out.dtype)
        gain_out[...] = jnp.sum(d * unit, axis=0, keepdims=True)

    return pl.pallas_call(
        kernel,
        in_specs=[pl.BlockSpec(memory_space=pltpu.VMEM)] * 6 + [ANYWHERE] * len(earlier),
        out_specs=[pl.BlockSpec(memory_space=pltpu.VMEM)] * 2,
        out_shape=[
            jax.ShapeDtypeStruct(grads.shape, grads.dtype),
            jax.ShapeDtypeStruct((1, grads.shape[1]), jnp.float32),
        ],
        cost_estimate=pl.CostEstimate(
            flops=8 * grads.size, bytes_accessed=8 * grads.size, transcendentals=0
        ),
        compiler_params=pltpu.CompilerParams(vmem_limit_bytes=VMEM_LIMIT),
    )(d_part, tokens, grads, inverse, row_mean, gain, *earlier)


def after(array, *earlier):
    def nothing(*refs):
        pass

    return pl.pallas_call(
        nothing,
        in_specs=[ANYWHERE] * (1 + len(earlier)),
        out_specs=ANYWHERE,
        out_shape=jax.ShapeDtypeStruct(array.shape, array.dtype),
        input_output_aliases={0: 0},
    )(array, *earlier)


def far_block(chunks, group):
    low, high = jnp.concatenate(chunks[:2]), jnp.concatenate(chunks[2:])
    return jnp.where(group == 0, jnp.concatenate([low, high]), jnp.concatenate([high, low]))


def fast_body(passages, cotangent, passage_counts, norm_gain, w_query, w_key, w_value, w_out):
    me = lax.axis_index("pas")
    group = lax.axis_index("grp")
    feature = lax.axis_index("fsdp")
    seq = passages.shape[1]
    pos = jnp.stack([me, group]).astype(jnp.int32)

    first_chunk = cut(w_key, group * 2, 256, ())

    counts = lax.all_gather(after(passage_counts, first_chunk), "pas", axis=0, tiled=True)
    index = jnp.arange(4, dtype=jnp.int32)
    single = counts == 1
    source = jnp.sum(jnp.where(counts == 4, index, 0))
    rank = lambda d: jnp.minimum(jnp.sum((single & (index < d)).astype(jnp.int32)), 1)
    host0 = jnp.min(jnp.where(single, index, 4))
    host1 = jnp.max(jnp.where(single, index, -1))
    own_count = passage_counts[0]
    relation = me ^ source

    def send_second(array):
        extra = array[2:4]
        extra_core = swap(extra, "pas", 1)
        there = rank(me ^ 2)
        picked = jnp.where(source == me, extra, extra_core)
        return extra_core, jnp.where(there == 0, picked[0], picked[1])

    def second(array, extra_core, got_x):
        from_core = jnp.where(rank(me) == 0, extra_core[0], extra_core[1])
        foreign = jnp.where(relation == 1, from_core, got_x)
        return jnp.where(own_count >= 2, array[1], foreign)

    weights = (w_key, w_query, w_value, w_out)
    over_x, over_y, cuts = [], [], []

    def send(*earlier):
        i = len(over_x)
        if i == 8:
            chunk = cut_ends(w_out, earlier)
        elif i == 7:
            chunk = cut(w_out, group * 4 + 2, 128, earlier)
        elif i == 0:
            chunk = first_chunk
        else:
            chunk = cut(weights[i // 2], group * 2 + i % 2, 256, earlier)
        cuts.append(chunk)
        over_x.append(swap(chunk, "pas", 2))

    def forward(*earlier):
        i = len(over_y)
        if earlier:
            over_x[i] = after(over_x[i], *earlier)
        over_y.append(swap(over_x[i], "grp", 1))

    def fetch(i):
        far = far_block(over_x[i : i + 2] + over_y[i : i + 2], group)
        return [weights[i // 2], swap(weights[i // 2], "pas", 1), far, swap(far, "pas", 1)]

    send()
    tokens_core, tokens_sent = send_second(passages)
    grads_core, grads_sent = send_second(cotangent)
    tokens_x = swap(tokens_sent, "pas", 2)
    grads_x = swap(grads_sent, "pas", 2)
    tokens = jnp.concatenate([passages[0], second(passages, tokens_core, tokens_x)], axis=0)
    send(tokens_sent)
    tokens = after(tokens, cuts[1])
    grads = jnp.concatenate([cotangent[0], second(cotangent, grads_core, grads_x)], axis=0)
    all_tokens = lax.all_gather(tokens, "fsdp", axis=0)
    all_grads = lax.all_gather(grads, "fsdp", axis=0)

    tokens_f32 = all_tokens.astype(jnp.float32)
    width = norm_gain.shape[0]
    gain = norm_gain.reshape(4, 1, 1024)
    inverse = lax.rsqrt(
        jnp.sum(tokens_f32 * tokens_f32, axis=(0, 2), keepdims=True) / width + EPSILON
    )
    normed = (tokens_f32 * inverse * gain).astype(jnp.bfloat16)

    rows_shape = jax.ShapeDtypeStruct((2 * seq, 1024), jnp.bfloat16)
    wide_shape = jax.ShapeDtypeStruct((4, 2 * seq, 1024), jnp.bfloat16)

    def project(w, *earlier):
        return call(project_kernel, pos, [normed], [w], rows_shape, *earlier)

    send(over_x[0], tokens_x)
    forward(cuts[2])
    send(over_x[1], grads_sent)
    forward(cuts[3])
    key_w = fetch(0)
    send(over_x[2], over_y[0])
    forward(cuts[4])
    send(over_x[3], over_y[1], grads)
    forward(cuts[5])
    query_w = fetch(2)
    send(over_x[4], over_y[2])
    forward(cuts[6])
    send(over_x[5], over_y[3])
    forward(cuts[7])
    send(over_x[6], over_y[4])
    forward(cuts[8])
    keys = project(key_w)
    query = project(query_w)
    over_x[8] = after(over_x[8], over_y[5], keys, query)
    forward()
    far = over_x[4:6] + over_y[4:6]
    value_w = [w_value, swap(w_value, "pas", 1), far, [swap(c, "pas", 1) for c in far]]
    far = over_x[6:9] + over_y[6:8]
    far_core = [swap(c, "pas", 1) for c in far]
    out_w = [w_out, swap(w_out, "pas", 1), far + far[2:3], far_core + far_core[2:3]]
    values = project(value_w, all_grads)
    (context,) = attend(attention_kernel, (query, keys, values), 1)
    partial_out = call(emit_kernel, pos, [context], [out_w], wide_shape)
    attention = lax.psum_scatter(partial_out, "fsdp", scatter_dimension=0)
    d_context = call(project_out_kernel, pos, [after(all_grads, partial_out)], [out_w], rows_shape)
    d_query, d_keys, d_values = attend(attention_back_kernel, (query, keys, values, d_context), 3)
    d_normed = call(
        back_kernel, pos, [d_query, d_keys, d_values], [query_w, key_w, value_w], wide_shape
    )

    d_normed = after(d_normed, attention)
    d_part = lax.psum_scatter(d_normed, "fsdp", scatter_dimension=0)

    row_total = jnp.sum(
        d_normed.astype(jnp.float32) * gain * (tokens_f32 * inverse), axis=(0, 2)
    ).reshape(2, seq)
    row_total += swap(row_total, "fsdp", 1)
    row_total += swap(row_total, "fsdp", 2)
    row_mean = row_total.reshape(2 * seq, 1) / width

    gain_part = lax.dynamic_slice_in_dim(norm_gain, feature * 1024, 1024, 0)
    states = (tokens.astype(jnp.float32) + attention.reshape(2 * seq, 1024).astype(jnp.float32)).astype(jnp.bfloat16)
    def home(local):
        local = local.reshape(2, seq, 1024)
        back = local[1]
        over_x = swap(back, "pas", 2)
        over_core = swap(jnp.stack([back, over_x]), "pas", 1)

        def pick(host):
            way = host ^ me
            return jnp.where(way == 1, over_core[0], jnp.where(way == 2, over_x, over_core[1]))

        zero = jnp.zeros_like(back)
        return jnp.stack(
            [
                local[0],
                jnp.where(own_count >= 2, back, zero),
                jnp.where(own_count == 4, pick(host0), zero),
                jnp.where(own_count == 4, pick(host1), zero),
            ]
        )

    encoded = home(states)
    input_local, gain_grad = finish(
        d_part.reshape(2 * seq, 1024),
        tokens,
        grads,
        inverse.reshape(2 * seq, 1),
        row_mean,
        gain_part.reshape(1, 1024),
        encoded,
    )
    input_grad = home(input_local)
    gain_grad = gain_grad.reshape(8, 128)
    gain_grad += swap(gain_grad, "pas", 1)
    gain_grad += swap(gain_grad, "pas", 2)
    return encoded, input_grad, gain_grad.reshape(1024)


def solution(mesh):
    placed = (
        P(("grp", "pas"), None, "fsdp"),
        P(("grp", "pas"), None, "fsdp"),
        P(("grp", "pas")),
        P(),
        P("pas", "fsdp"),
        P("pas", "fsdp"),
        P("pas", "fsdp"),
        P("fsdp", "pas"),
    )
    sizes = dict(mesh.shape)
    fast = sizes["grp"] == 2 and sizes["pas"] == 4 and sizes["fsdp"] == 4
    return jax.shard_map(
        fast_body if fast else general_body,
        mesh=mesh,
        in_specs=placed,
        out_specs=(
            P(("grp", "pas"), None, "fsdp"),
            P(("grp", "pas"), None, "fsdp"),
            P(("grp", "fsdp")),
        ),
        check_vma=False,
    )
```

```python
import jax
import jax.numpy as jnp
from jax import lax
from jax.experimental import pallas as pl
from jax.experimental.pallas import tpu as pltpu
from jax.sharding import PartitionSpec as P

HD = 64
BAL = 2
EPSILON = 1e-06
VMEM_LIMIT = 50 * 2**20
LITTLE = pl.CostEstimate(flops=1, bytes_accessed=1, transcendentals=0)


def entering(shard, axis, combine, identity):
    length, position = (lax.axis_size(axis), lax.axis_index(axis))
    everything = lax.all_gather(shard, axis)
    start = jnp.broadcast_to(jnp.asarray(identity, shard.dtype), shard.shape)

    def lap(k, before):
        reached = k < position
        new = combine(before, everything[k])
        return jnp.where(reached, new, before)

    return lax.fori_loop(0, length, lap, start)


def add_counts(earlier, later):
    return earlier + later


def general_body(passages, cotangent, passage_counts, norm_gain, w_query, w_key, w_value, w_out):
    peer_total = lax.axis_size("pas")
    slots, seq_len, part_width = passages.shape
    flat_width = seq_len * part_width
    own_count = passage_counts[0]
    first_rank = entering(passage_counts, "pas", add_counts, jnp.zeros_like(passage_counts))[0]
    slot_index = jnp.arange(slots, dtype=jnp.int32)
    slot_rank = first_rank + slot_index
    is_live = slot_index < own_count
    peer_index = jnp.arange(peer_total, dtype=jnp.int32)
    routing_mask = is_live[None, :] & ((slot_rank % peer_total)[None, :] == peer_index[:, None])
    routing = routing_mask.astype(jnp.bfloat16)
    sent_rank = jnp.max(jnp.where(routing_mask, slot_rank[None, :], -1), axis=1).astype(jnp.int32)
    send_tokens = jnp.dot(
        routing, passages.reshape(slots, flat_width), preferred_element_type=jnp.float32
    ).astype(jnp.bfloat16)
    send_grads = jnp.dot(
        routing, cotangent.reshape(slots, flat_width), preferred_element_type=jnp.float32
    ).astype(jnp.bfloat16)
    got_tokens, got_grads, got_rank = (
        lax.all_to_all(send_tokens, "pas", split_axis=0, concat_axis=0, tiled=True),
        lax.all_to_all(send_grads, "pas", split_axis=0, concat_axis=0, tiled=True),
        lax.all_to_all(sent_rank, "pas", split_axis=0, concat_axis=0, tiled=True),
    )
    picked_mask = (got_rank[None, :] >= 0) & (
        got_rank[None, :] // peer_total == jnp.arange(BAL, dtype=jnp.int32)[:, None]
    )
    picked = picked_mask.astype(jnp.bfloat16)
    returned = jnp.transpose(picked)
    local_tokens = (
        jnp.dot(picked, got_tokens, preferred_element_type=jnp.float32)
        .astype(jnp.bfloat16)
        .reshape(BAL, seq_len, part_width)
    )
    local_grads = (
        jnp.dot(picked, got_grads, preferred_element_type=jnp.float32)
        .astype(jnp.bfloat16)
        .reshape(BAL, seq_len, part_width)
    )
    query_w, key_w, value_w, out_w = (
        lax.all_gather(w_query, "pas", axis=0, tiled=True),
        lax.all_gather(w_key, "pas", axis=0, tiled=True),
        lax.all_gather(w_value, "pas", axis=0, tiled=True),
        lax.all_gather(w_out, "pas", axis=1, tiled=True),
    )
    full_tokens = lax.all_gather(local_tokens, "fsdp", axis=2, tiled=True)
    width = full_tokens.shape[2]
    feature_start = lax.axis_index("fsdp") * part_width
    full_f32 = full_tokens.astype(jnp.float32)
    inverse = lax.rsqrt(jnp.mean(full_f32 * full_f32, axis=-1, keepdims=True) + EPSILON)
    unit_rows = full_f32 * inverse
    normed = (unit_rows * norm_gain).astype(jnp.bfloat16)
    local_cols = query_w.shape[1]
    head_count = local_cols // HD
    flat_rows = normed.reshape(BAL * seq_len, width)

    def project(weight):
        result = jnp.dot(flat_rows, weight, preferred_element_type=jnp.float32).astype(jnp.bfloat16)
        return result.reshape(BAL, seq_len, head_count, HD)

    query = project(query_w)
    keys = project(key_w)
    values = project(value_w)
    scores = jnp.einsum("blhe,bmhe->bhlm", query, keys, preferred_element_type=jnp.float32)
    probs = jax.nn.softmax(scores, axis=-1)
    probs_low = probs.astype(jnp.bfloat16)
    context = jnp.einsum(
        "bhlm,bmhe->blhe", probs_low, values, preferred_element_type=jnp.float32
    ).astype(jnp.bfloat16)
    context_rows = context.reshape(BAL * seq_len, local_cols)
    partial_out = jnp.dot(context_rows, out_w, preferred_element_type=jnp.float32).reshape(
        BAL, seq_len, width
    )
    attention = lax.psum_scatter(
        partial_out.astype(jnp.bfloat16), "fsdp", scatter_dimension=2, tiled=True
    ).astype(jnp.float32)
    states = (local_tokens.astype(jnp.float32) + attention).astype(jnp.bfloat16)
    states_back = jnp.dot(
        returned, states.reshape(BAL, flat_width), preferred_element_type=jnp.float32
    ).astype(jnp.bfloat16)
    states_home = lax.all_to_all(states_back, "pas", split_axis=0, concat_axis=0, tiled=True)
    upstream_rows = lax.all_gather(local_grads, "fsdp", axis=2, tiled=True).reshape(
        BAL * seq_len, width
    )
    d_context = jnp.einsum(
        "td,cd->tc", upstream_rows, out_w, preferred_element_type=jnp.float32
    ).astype(jnp.bfloat16)
    d_context = d_context.reshape(BAL, seq_len, head_count, HD)
    d_values = jnp.einsum(
        "bhlm,blhe->bmhe", probs_low, d_context, preferred_element_type=jnp.float32
    ).astype(jnp.bfloat16)
    d_probs = jnp.einsum("blhe,bmhe->bhlm", d_context, values, preferred_element_type=jnp.float32)
    d_scores = (probs * (d_probs - jnp.sum(d_probs * probs, axis=-1, keepdims=True))).astype(
        jnp.bfloat16
    )
    d_query = jnp.einsum(
        "bhlm,bmhe->blhe", d_scores, keys, preferred_element_type=jnp.float32
    ).astype(jnp.bfloat16)
    d_keys = jnp.einsum(
        "bhlm,blhe->bmhe", d_scores, query, preferred_element_type=jnp.float32
    ).astype(jnp.bfloat16)

    def back_project(grad, weight):
        grad_rows = grad.reshape(BAL * seq_len, local_cols)
        return jnp.einsum("tc,dc->td", grad_rows, weight, preferred_element_type=jnp.float32)

    d_normed = (
        back_project(d_query, query_w)
        + back_project(d_keys, key_w)
        + back_project(d_values, value_w)
    )
    d_normed_part = lax.psum_scatter(
        d_normed.reshape(BAL, seq_len, width).astype(jnp.bfloat16),
        "fsdp",
        scatter_dimension=2,
        tiled=True,
    ).astype(jnp.float32)
    unit_part = lax.dynamic_slice_in_dim(unit_rows, feature_start, part_width, 2)
    gain_part = lax.dynamic_slice_in_dim(norm_gain, feature_start, part_width, 0)
    d_unit = d_normed_part * gain_part
    row_total = lax.psum(jnp.sum(d_unit * unit_part, axis=-1, keepdims=True), "fsdp")
    row_mean = row_total / width
    d_tokens = inverse * (d_unit - unit_part * row_mean)
    grads_local = (local_grads.astype(jnp.float32) + d_tokens).astype(jnp.bfloat16)
    gain_grad = lax.psum(jnp.sum(d_normed_part * unit_part, axis=(0, 1)), "pas")
    grads_back = jnp.dot(
        returned, grads_local.reshape(BAL, flat_width), preferred_element_type=jnp.float32
    ).astype(jnp.bfloat16)
    grads_home = lax.all_to_all(grads_back, "pas", split_axis=0, concat_axis=0, tiled=True)
    routing_back = jnp.transpose(routing)
    encoded = (
        jnp.dot(routing_back, states_home, preferred_element_type=jnp.float32)
        .astype(jnp.bfloat16)
        .reshape(slots, seq_len, part_width)
    )
    input_grad = (
        jnp.dot(routing_back, grads_home, preferred_element_type=jnp.float32)
        .astype(jnp.bfloat16)
        .reshape(slots, seq_len, part_width)
    )
    return (encoded, input_grad, gain_grad)


ANYWHERE = pl.BlockSpec(memory_space=pl.ANY)


def swap(array, axis, bit):
    return lax.ppermute(array, axis, [(i, i ^ bit) for i in range(lax.axis_size(axis))])


def dot_nn(a, b):
    return jnp.dot(a, b, preferred_element_type=jnp.float32)


def dot_nt(a, b):
    return lax.dot_general(a, b, (((1,), (1,)), ((), ())), preferred_element_type=jnp.float32)


def dot_tn(a, b):
    return lax.dot_general(a, b, (((0,), (0,)), ((), ())), preferred_element_type=jnp.float32)


def places(group, count):
    first, second = group * 512, (1 - group) * 512
    if count == 4:
        rows = [first, first + 256, second, second + 256]
    else:
        rows = [first, first + 256, 384, second, second + 256, 896]
    return [pl.multiple_of(r, 128) for r in rows]


def stream(weights, pos, held, sems):
    started = {}
    for i in range(4):
        for w, pieces in enumerate(weights):
            piece = pieces[i]
            if isinstance(piece, list):
                parts = []
                for j, (chunk, at) in enumerate(zip(piece, places(pos[1], len(piece)))):
                    size = 128 if len(piece) == 6 and j % 3 else 256
                    source = chunk
                    if j == 5:
                        source = chunk.at[pl.ds(128, 128)]
                    elif len(piece) == 6 and j == 2:
                        source = chunk.at[pl.ds(0, 128)]
                    parts.append((source, held.at[w, i, pl.ds(at, size)], sems.at[w, i, j]))
            else:
                parts = [(piece, held.at[w, i], sems.at[w, i, 0])]
            started[w, i] = [pltpu.make_async_copy(*part) for part in parts]
            for copy in started[w, i]:
                copy.start()

    def ready(w, i):
        for copy in started[w, i]:
            copy.wait()
        return held.at[w, i]

    return ready


TILES = [pl.ds(256 * t, 256) for t in range(4)]


def project_kernel(weights, pos, dense, out, held, sems):
    ready = stream(weights, pos, held, sems)
    totals = [0.0] * 4
    for i in range(4):
        block = ready(0, i)
        rows = dense[0][pos[0] ^ i]
        for t, tile in enumerate(TILES):
            totals[t] += dot_nn(rows, block[:, tile])
    for total, tile in zip(totals, TILES):
        out[:, tile] = total.astype(out.dtype)


def project_out_kernel(weights, pos, dense, out, held, sems):
    ready = stream(weights, pos, held, sems)
    totals = [0.0] * 4
    for i in range(4):
        block = ready(0, i)
        rows = dense[0][pos[0] ^ i]
        for t, tile in enumerate(TILES):
            totals[t] += dot_nt(rows, block[tile])
    for total, tile in zip(totals, TILES):
        out[:, tile] = total.astype(out.dtype)


def emit_kernel(weights, pos, dense, out, held, sems):
    ready = stream(weights, pos, held, sems)
    rows = dense[0][...]
    for i in range(4):
        block = ready(0, i)
        for tile in TILES:
            out[pos[0] ^ i, :, tile] = dot_nn(rows, block[:, tile]).astype(out.dtype)


def back_kernel(weights, pos, dense, out, held, sems):
    ready = stream(weights, pos, held, sems)
    grads = [d[...] for d in dense]
    for i in range(4):
        blocks = [ready(w, i) for w in range(3)]
        for tile in TILES:
            total = sum(dot_nt(g, block[tile]) for g, block in zip(grads, blocks))
            out[pos[0] ^ i, :, tile] = total.astype(out.dtype)


def call(kernel, pos, dense, weights, out_shape, *earlier):
    flat, tree = jax.tree.flatten(weights)
    count = len(weights)

    def run(pos_ref, *refs):
        dense_refs = refs[: len(dense)]
        weight_refs = jax.tree.unflatten(tree, refs[len(dense) : len(dense) + len(flat)])
        out, held, sems = refs[-3:]
        kernel(weight_refs, pos_ref, dense_refs, out, held, sems)

    size = count * 2**22
    return pl.pallas_call(
        run,
        in_specs=[pl.BlockSpec(memory_space=pltpu.SMEM)]
        + [pl.BlockSpec(memory_space=pltpu.VMEM)] * len(dense)
        + [ANYWHERE] * (len(flat) + len(earlier)),
        out_specs=pl.BlockSpec(memory_space=pltpu.VMEM),
        out_shape=out_shape,
        scratch_shapes=[
            pltpu.VMEM((count, 4, 1024, 1024), jnp.bfloat16),
            pltpu.SemaphoreType.DMA((count, 4, 6)),
        ],
        cost_estimate=LITTLE,
        compiler_params=pltpu.CompilerParams(vmem_limit_bytes=(8 * count + 8) * 2**20),
    )(pos, *dense, *flat, *earlier)


def head_pairs(width):
    return [pl.ds(pair * 128, 128) for pair in range(width // 128)]


def first_head(seq):
    return lax.broadcasted_iota(jnp.int32, (seq, 128), 1) < HD


def split_heads(array):
    first = first_head(array.shape[0])
    mask0 = jnp.where(first, 1.0, 0.0).astype(array.dtype)
    mask1 = jnp.where(first, 0.0, 1.0).astype(array.dtype)
    return jnp.concatenate([array * mask0, array * mask1], axis=0)


def join_heads(both):
    seq = both.shape[0] // 2
    return jnp.where(first_head(seq), both[:seq], both[seq:])


def softmax_pair(scores):
    seq = scores.shape[0]
    probs = []
    for h in range(2):
        s = scores[:, h * seq : (h + 1) * seq]
        e = jnp.exp(s - jnp.max(s, axis=-1, keepdims=True))
        probs.append(e / jnp.sum(e, axis=-1, keepdims=True))
    return probs


def attention_kernel(q_ref, k_ref, v_ref, ctx_ref):
    for at in head_pairs(q_ref.shape[1]):
        probs = softmax_pair(dot_nt(q_ref[:, at], split_heads(k_ref[:, at])))
        low = jnp.concatenate([p.astype(jnp.bfloat16) for p in probs], axis=1)
        ctx_ref[:, at] = dot_nn(low, split_heads(v_ref[:, at])).astype(jnp.bfloat16)


def attention_back_kernel(q_ref, k_ref, v_ref, dc_ref, dq_ref, dk_ref, dv_ref):
    seq = q_ref.shape[0]
    for at in head_pairs(q_ref.shape[1]):
        q, dc = q_ref[:, at], dc_ref[:, at]
        keys = split_heads(k_ref[:, at])
        probs = softmax_pair(dot_nt(q, keys))
        d_probs = dot_nt(dc, split_heads(v_ref[:, at]))
        d_scores = []
        for h in range(2):
            dp = d_probs[:, h * seq : (h + 1) * seq]
            ds = probs[h] * (dp - jnp.sum(dp * probs[h], axis=-1, keepdims=True))
            d_scores.append(ds.astype(jnp.bfloat16))
        low = jnp.concatenate([p.astype(jnp.bfloat16) for p in probs], axis=1)
        ds = jnp.concatenate(d_scores, axis=1)
        dq_ref[:, at] = dot_nn(ds, keys).astype(jnp.bfloat16)
        dv_ref[:, at] = join_heads(dot_tn(low, dc)).astype(jnp.bfloat16)
        dk_ref[:, at] = join_heads(dot_tn(ds, q)).astype(jnp.bfloat16)


def attend(kernel, arrays, outputs):
    rows, cols = arrays[0].shape
    spec = pl.BlockSpec((rows // BAL, cols // 2), lambda i, j: (i, j))
    shape = jax.ShapeDtypeStruct((rows, cols), jnp.bfloat16)
    many = len(arrays) + outputs
    return pl.pallas_call(
        kernel,
        grid=(BAL, 2),
        in_specs=[spec] * len(arrays),
        out_specs=[spec] * outputs,
        out_shape=[shape] * outputs,
        cost_estimate=LITTLE,
        compiler_params=pltpu.CompilerParams(vmem_limit_bytes=VMEM_LIMIT),
    )(*arrays)


def cut(weight, block, rows, earlier):
    def copy(block_ref, source, *refs):
        refs[-1][...] = source[...]

    return pl.pallas_call(
        copy,
        grid_spec=pltpu.PrefetchScalarGridSpec(
            num_scalar_prefetch=1,
            grid=(1,),
            in_specs=[pl.BlockSpec((rows, 1024), lambda i, block: (block[0], 0))]
            + [ANYWHERE] * len(earlier),
            out_specs=pl.BlockSpec((rows, 1024), lambda i, block: (0, 0)),
        ),
        out_shape=jax.ShapeDtypeStruct((rows, 1024), weight.dtype),
        cost_estimate=LITTLE,
    )(block.reshape(1), weight, *earlier)


def cut_ends(weight, earlier):
    def copy(low, high, *refs):
        refs[-1][0:128] = low[...]
        refs[-1][128:256] = high[...]

    return pl.pallas_call(
        copy,
        grid=(1,),
        in_specs=[
            pl.BlockSpec((128, 1024), lambda i: (3, 0)),
            pl.BlockSpec((128, 1024), lambda i: (7, 0)),
        ]
        + [ANYWHERE] * len(earlier),
        out_specs=pl.BlockSpec((256, 1024), lambda i: (0, 0)),
        out_shape=jax.ShapeDtypeStruct((256, 1024), weight.dtype),
        cost_estimate=LITTLE,
    )(weight, weight, *earlier)


def finish(d_part, tokens, grads, inverse, row_mean, gain, *earlier):
    def kernel(d_ref, x_ref, g_ref, inverse_ref, mean_ref, gain_ref, *refs):
        grad_out, gain_out = refs[-2:]
        d = d_ref[...].astype(jnp.float32)
        scale = inverse_ref[...]
        unit = x_ref[...].astype(jnp.float32) * scale
        d_tokens = scale * (d * gain_ref[...] - unit * mean_ref[...])
        grad_out[...] = (g_ref[...].astype(jnp.float32) + d_tokens).astype(grad_out.dtype)
        gain_out[...] = jnp.sum(d * unit, axis=0, keepdims=True)

    return pl.pallas_call(
        kernel,
        in_specs=[pl.BlockSpec(memory_space=pltpu.VMEM)] * 6 + [ANYWHERE] * len(earlier),
        out_specs=[pl.BlockSpec(memory_space=pltpu.VMEM)] * 2,
        out_shape=[
            jax.ShapeDtypeStruct(grads.shape, grads.dtype),
            jax.ShapeDtypeStruct((1, grads.shape[1]), jnp.float32),
        ],
        cost_estimate=LITTLE,
        compiler_params=pltpu.CompilerParams(vmem_limit_bytes=VMEM_LIMIT),
    )(d_part, tokens, grads, inverse, row_mean, gain, *earlier)


def after(array, *earlier):
    def nothing(*refs):
        pass

    return pl.pallas_call(
        nothing,
        in_specs=[ANYWHERE] * (1 + len(earlier)),
        out_specs=ANYWHERE,
        out_shape=jax.ShapeDtypeStruct(array.shape, array.dtype),
        input_output_aliases={0: 0},
    )(array, *earlier)


def far_block(chunks, group):
    low, high = jnp.concatenate(chunks[:2]), jnp.concatenate(chunks[2:])
    return jnp.where(group == 0, jnp.concatenate([low, high]), jnp.concatenate([high, low]))


def fast_body(passages, cotangent, passage_counts, norm_gain, w_query, w_key, w_value, w_out):
    me = lax.axis_index("pas")
    group = lax.axis_index("grp")
    feature = lax.axis_index("fsdp")
    seq = passages.shape[1]
    pos = jnp.stack([me, group]).astype(jnp.int32)

    first_chunk = cut(w_key, group * 2, 256, ())

    counts = lax.all_gather(after(passage_counts, first_chunk), "pas", axis=0, tiled=True)
    index = jnp.arange(4, dtype=jnp.int32)
    single = counts == 1
    source = jnp.sum(jnp.where(counts == 4, index, 0))
    rank = lambda d: jnp.minimum(jnp.sum((single & (index < d)).astype(jnp.int32)), 1)
    host0 = jnp.min(jnp.where(single, index, 4))
    host1 = jnp.max(jnp.where(single, index, -1))
    own_count = passage_counts[0]
    relation = me ^ source

    def send_second(array):
        extra = array[2:4]
        extra_core = swap(extra, "pas", 1)
        there = rank(me ^ 2)
        picked = jnp.where(source == me, extra, extra_core)
        return extra_core, jnp.where(there == 0, picked[0], picked[1])

    def second(array, extra_core, got_x):
        from_core = jnp.where(rank(me) == 0, extra_core[0], extra_core[1])
        foreign = jnp.where(relation == 1, from_core, got_x)
        return jnp.where(own_count >= 2, array[1], foreign)

    weights = (w_key, w_query, w_value, w_out)
    over_x, over_y, cuts = [], [], []

    def send(*earlier):
        i = len(over_x)
        if i == 8:
            chunk = cut_ends(w_out, earlier)
        elif i == 7:
            chunk = cut(w_out, group * 4 + 2, 128, earlier)
        elif i == 0:
            chunk = first_chunk
        else:
            chunk = cut(weights[i // 2], group * 2 + i % 2, 256, earlier)
        cuts.append(chunk)
        over_x.append(swap(chunk, "pas", 2))

    def forward(*earlier):
        i = len(over_y)
        if earlier:
            over_x[i] = after(over_x[i], *earlier)
        over_y.append(swap(over_x[i], "grp", 1))

    def fetch(i):
        far = far_block(over_x[i : i + 2] + over_y[i : i + 2], group)
        return [weights[i // 2], swap(weights[i // 2], "pas", 1), far, swap(far, "pas", 1)]

    send()
    tokens_core, tokens_sent = send_second(passages)
    grads_core, grads_sent = send_second(cotangent)
    tokens_x = swap(tokens_sent, "pas", 2)
    grads_x = swap(grads_sent, "pas", 2)
    tokens = jnp.concatenate([passages[0], second(passages, tokens_core, tokens_x)], axis=0)
    send(tokens_sent)
    tokens = after(tokens, cuts[1])
    grads = jnp.concatenate([cotangent[0], second(cotangent, grads_core, grads_x)], axis=0)
    all_tokens = lax.all_gather(tokens, "fsdp", axis=0)
    all_grads = lax.all_gather(grads, "fsdp", axis=0)

    tokens_f32 = all_tokens.astype(jnp.float32)
    width = norm_gain.shape[0]
    gain = norm_gain.reshape(4, 1, 1024)
    inverse = lax.rsqrt(
        jnp.sum(tokens_f32 * tokens_f32, axis=(0, 2), keepdims=True) / width + EPSILON
    )
    normed = (tokens_f32 * inverse * gain).astype(jnp.bfloat16)

    rows_shape = jax.ShapeDtypeStruct((2 * seq, 1024), jnp.bfloat16)
    wide_shape = jax.ShapeDtypeStruct((4, 2 * seq, 1024), jnp.bfloat16)

    def project(w, *earlier):
        return call(project_kernel, pos, [normed], [w], rows_shape, *earlier)

    send(over_x[0], tokens_x)
    forward(cuts[2])
    send(over_x[1], grads_sent)
    forward(cuts[3])
    key_w = fetch(0)
    send(over_x[2], over_y[0])
    forward(cuts[4])
    send(over_x[3], over_y[1], grads)
    forward(cuts[5])
    query_w = fetch(2)
    send(over_x[4], over_y[2])
    forward(cuts[6])
    send(over_x[5], over_y[3])
    forward(cuts[7])
    send(over_x[6], over_y[4])
    keys = project(key_w)
    forward(cuts[8], keys)
    query = project(query_w, all_grads)
    over_x[8] = after(over_x[8], over_y[5], query)
    forward()
    far = over_x[4:6] + over_y[4:6]
    value_w = [w_value, swap(w_value, "pas", 1), far, [swap(c, "pas", 1) for c in far]]
    far = over_x[6:9] + over_y[6:8]
    far_core = [swap(c, "pas", 1) for c in far]
    out_w = [w_out, swap(w_out, "pas", 1), far + far[2:3], far_core + far_core[2:3]]
    values = project(value_w)
    (context,) = attend(attention_kernel, (query, keys, values), 1)
    partial_out = call(emit_kernel, pos, [context], [out_w], wide_shape)
    attention = lax.psum_scatter(partial_out, "fsdp", scatter_dimension=0)
    d_context = call(project_out_kernel, pos, [after(all_grads, partial_out)], [out_w], rows_shape)
    d_query, d_keys, d_values = attend(attention_back_kernel, (query, keys, values, d_context), 3)
    d_normed = call(
        back_kernel, pos, [d_query, d_keys, d_values], [query_w, key_w, value_w], wide_shape
    )

    d_normed = after(d_normed, attention)
    d_part = lax.psum_scatter(d_normed, "fsdp", scatter_dimension=0)

    row_total = jnp.sum(
        d_normed.astype(jnp.float32) * gain * (tokens_f32 * inverse), axis=(0, 2)
    ).reshape(2, seq)
    row_total += swap(row_total, "fsdp", 1)
    row_total += swap(row_total, "fsdp", 2)
    row_mean = row_total.reshape(2 * seq, 1) / width

    gain_part = lax.dynamic_slice_in_dim(norm_gain, feature * 1024, 1024, 0)
    states = (tokens.astype(jnp.float32) + attention.reshape(2 * seq, 1024).astype(jnp.float32)).astype(jnp.bfloat16)
    def home(local):
        local = local.reshape(2, seq, 1024)
        back = local[1]
        over_x = swap(back, "pas", 2)
        over_core = swap(back, "pas", 1)
        over_both = swap(over_x, "pas", 1)

        def pick(host):
            way = host ^ me
            return jnp.where(way == 1, over_core, jnp.where(way == 2, over_x, over_both))

        zero = jnp.zeros_like(back)
        return jnp.stack(
            [
                local[0],
                jnp.where(own_count >= 2, back, zero),
                jnp.where(own_count == 4, pick(host0), zero),
                jnp.where(own_count == 4, pick(host1), zero),
            ]
        )

    encoded = home(states)
    input_local, gain_grad = finish(
        d_part.reshape(2 * seq, 1024),
        tokens,
        grads,
        inverse.reshape(2 * seq, 1),
        row_mean,
        gain_part.reshape(1, 1024),
        encoded,
    )
    input_grad = home(input_local)
    gain_grad = gain_grad.reshape(8, 128)
    others = [swap(gain_grad, "pas", bits) for bits in (1, 2, 3)]
    gain_grad = (gain_grad + others[0]) + (others[1] + others[2])
    return encoded, input_grad, gain_grad.reshape(1024)


def solution(mesh):
    placed = (
        P(("grp", "pas"), None, "fsdp"),
        P(("grp", "pas"), None, "fsdp"),
        P(("grp", "pas")),
        P(),
        P("pas", "fsdp"),
        P("pas", "fsdp"),
        P("pas", "fsdp"),
        P("fsdp", "pas"),
    )
    sizes = dict(mesh.shape)
    fast = sizes["grp"] == 2 and sizes["pas"] == 4 and sizes["fsdp"] == 4
    return jax.shard_map(
        fast_body if fast else general_body,
        mesh=mesh,
        in_specs=placed,
        out_specs=(
            P(("grp", "pas"), None, "fsdp"),
            P(("grp", "pas"), None, "fsdp"),
            P(("grp", "fsdp")),
        ),
        check_vma=False,
    )
```

```python
import jax
import jax.numpy as jnp
from jax import lax
from jax.experimental import pallas as pl
from jax.experimental.pallas import tpu as pltpu
from jax.sharding import PartitionSpec as P

HD = 64
BAL = 2
EPSILON = 1e-06
VMEM_LIMIT = 50 * 2**20
LITTLE = pl.CostEstimate(flops=1, bytes_accessed=1, transcendentals=0)


def entering(shard, axis, combine, identity):
    length, position = (lax.axis_size(axis), lax.axis_index(axis))
    everything = lax.all_gather(shard, axis)
    start = jnp.broadcast_to(jnp.asarray(identity, shard.dtype), shard.shape)

    def lap(k, before):
        reached = k < position
        new = combine(before, everything[k])
        return jnp.where(reached, new, before)

    return lax.fori_loop(0, length, lap, start)


def add_counts(earlier, later):
    return earlier + later


def general_body(passages, cotangent, passage_counts, norm_gain, w_query, w_key, w_value, w_out):
    peer_total = lax.axis_size("pas")
    slots, seq_len, part_width = passages.shape
    flat_width = seq_len * part_width
    own_count = passage_counts[0]
    first_rank = entering(passage_counts, "pas", add_counts, jnp.zeros_like(passage_counts))[0]
    slot_index = jnp.arange(slots, dtype=jnp.int32)
    slot_rank = first_rank + slot_index
    is_live = slot_index < own_count
    peer_index = jnp.arange(peer_total, dtype=jnp.int32)
    routing_mask = is_live[None, :] & ((slot_rank % peer_total)[None, :] == peer_index[:, None])
    routing = routing_mask.astype(jnp.bfloat16)
    sent_rank = jnp.max(jnp.where(routing_mask, slot_rank[None, :], -1), axis=1).astype(jnp.int32)
    send_tokens = jnp.dot(
        routing, passages.reshape(slots, flat_width), preferred_element_type=jnp.float32
    ).astype(jnp.bfloat16)
    send_grads = jnp.dot(
        routing, cotangent.reshape(slots, flat_width), preferred_element_type=jnp.float32
    ).astype(jnp.bfloat16)
    got_tokens, got_grads, got_rank = (
        lax.all_to_all(send_tokens, "pas", split_axis=0, concat_axis=0, tiled=True),
        lax.all_to_all(send_grads, "pas", split_axis=0, concat_axis=0, tiled=True),
        lax.all_to_all(sent_rank, "pas", split_axis=0, concat_axis=0, tiled=True),
    )
    picked_mask = (got_rank[None, :] >= 0) & (
        got_rank[None, :] // peer_total == jnp.arange(BAL, dtype=jnp.int32)[:, None]
    )
    picked = picked_mask.astype(jnp.bfloat16)
    returned = jnp.transpose(picked)
    local_tokens = (
        jnp.dot(picked, got_tokens, preferred_element_type=jnp.float32)
        .astype(jnp.bfloat16)
        .reshape(BAL, seq_len, part_width)
    )
    local_grads = (
        jnp.dot(picked, got_grads, preferred_element_type=jnp.float32)
        .astype(jnp.bfloat16)
        .reshape(BAL, seq_len, part_width)
    )
    query_w, key_w, value_w, out_w = (
        lax.all_gather(w_query, "pas", axis=0, tiled=True),
        lax.all_gather(w_key, "pas", axis=0, tiled=True),
        lax.all_gather(w_value, "pas", axis=0, tiled=True),
        lax.all_gather(w_out, "pas", axis=1, tiled=True),
    )
    full_tokens = lax.all_gather(local_tokens, "fsdp", axis=2, tiled=True)
    width = full_tokens.shape[2]
    feature_start = lax.axis_index("fsdp") * part_width
    full_f32 = full_tokens.astype(jnp.float32)
    inverse = lax.rsqrt(jnp.mean(full_f32 * full_f32, axis=-1, keepdims=True) + EPSILON)
    unit_rows = full_f32 * inverse
    normed = (unit_rows * norm_gain).astype(jnp.bfloat16)
    local_cols = query_w.shape[1]
    head_count = local_cols // HD
    flat_rows = normed.reshape(BAL * seq_len, width)

    def project(weight):
        result = jnp.dot(flat_rows, weight, preferred_element_type=jnp.float32).astype(jnp.bfloat16)
        return result.reshape(BAL, seq_len, head_count, HD)

    query = project(query_w)
    keys = project(key_w)
    values = project(value_w)
    scores = jnp.einsum("blhe,bmhe->bhlm", query, keys, preferred_element_type=jnp.float32)
    probs = jax.nn.softmax(scores, axis=-1)
    probs_low = probs.astype(jnp.bfloat16)
    context = jnp.einsum(
        "bhlm,bmhe->blhe", probs_low, values, preferred_element_type=jnp.float32
    ).astype(jnp.bfloat16)
    context_rows = context.reshape(BAL * seq_len, local_cols)
    partial_out = jnp.dot(context_rows, out_w, preferred_element_type=jnp.float32).reshape(
        BAL, seq_len, width
    )
    attention = lax.psum_scatter(
        partial_out.astype(jnp.bfloat16), "fsdp", scatter_dimension=2, tiled=True
    ).astype(jnp.float32)
    states = (local_tokens.astype(jnp.float32) + attention).astype(jnp.bfloat16)
    states_back = jnp.dot(
        returned, states.reshape(BAL, flat_width), preferred_element_type=jnp.float32
    ).astype(jnp.bfloat16)
    states_home = lax.all_to_all(states_back, "pas", split_axis=0, concat_axis=0, tiled=True)
    upstream_rows = lax.all_gather(local_grads, "fsdp", axis=2, tiled=True).reshape(
        BAL * seq_len, width
    )
    d_context = jnp.einsum(
        "td,cd->tc", upstream_rows, out_w, preferred_element_type=jnp.float32
    ).astype(jnp.bfloat16)
    d_context = d_context.reshape(BAL, seq_len, head_count, HD)
    d_values = jnp.einsum(
        "bhlm,blhe->bmhe", probs_low, d_context, preferred_element_type=jnp.float32
    ).astype(jnp.bfloat16)
    d_probs = jnp.einsum("blhe,bmhe->bhlm", d_context, values, preferred_element_type=jnp.float32)
    d_scores = (probs * (d_probs - jnp.sum(d_probs * probs, axis=-1, keepdims=True))).astype(
        jnp.bfloat16
    )
    d_query = jnp.einsum(
        "bhlm,bmhe->blhe", d_scores, keys, preferred_element_type=jnp.float32
    ).astype(jnp.bfloat16)
    d_keys = jnp.einsum(
        "bhlm,blhe->bmhe", d_scores, query, preferred_element_type=jnp.float32
    ).astype(jnp.bfloat16)

    def back_project(grad, weight):
        grad_rows = grad.reshape(BAL * seq_len, local_cols)
        return jnp.einsum("tc,dc->td", grad_rows, weight, preferred_element_type=jnp.float32)

    d_normed = (
        back_project(d_query, query_w)
        + back_project(d_keys, key_w)
        + back_project(d_values, value_w)
    )
    d_normed_part = lax.psum_scatter(
        d_normed.reshape(BAL, seq_len, width).astype(jnp.bfloat16),
        "fsdp",
        scatter_dimension=2,
        tiled=True,
    ).astype(jnp.float32)
    unit_part = lax.dynamic_slice_in_dim(unit_rows, feature_start, part_width, 2)
    gain_part = lax.dynamic_slice_in_dim(norm_gain, feature_start, part_width, 0)
    d_unit = d_normed_part * gain_part
    row_total = lax.psum(jnp.sum(d_unit * unit_part, axis=-1, keepdims=True), "fsdp")
    row_mean = row_total / width
    d_tokens = inverse * (d_unit - unit_part * row_mean)
    grads_local = (local_grads.astype(jnp.float32) + d_tokens).astype(jnp.bfloat16)
    gain_grad = lax.psum(jnp.sum(d_normed_part * unit_part, axis=(0, 1)), "pas")
    grads_back = jnp.dot(
        returned, grads_local.reshape(BAL, flat_width), preferred_element_type=jnp.float32
    ).astype(jnp.bfloat16)
    grads_home = lax.all_to_all(grads_back, "pas", split_axis=0, concat_axis=0, tiled=True)
    routing_back = jnp.transpose(routing)
    encoded = (
        jnp.dot(routing_back, states_home, preferred_element_type=jnp.float32)
        .astype(jnp.bfloat16)
        .reshape(slots, seq_len, part_width)
    )
    input_grad = (
        jnp.dot(routing_back, grads_home, preferred_element_type=jnp.float32)
        .astype(jnp.bfloat16)
        .reshape(slots, seq_len, part_width)
    )
    return (encoded, input_grad, gain_grad)


ANYWHERE = pl.BlockSpec(memory_space=pl.ANY)


def swap(array, axis, bit):
    return lax.ppermute(array, axis, [(i, i ^ bit) for i in range(lax.axis_size(axis))])


def dot_nn(a, b):
    return jnp.dot(a, b, preferred_element_type=jnp.float32)


def dot_nt(a, b):
    return lax.dot_general(a, b, (((1,), (1,)), ((), ())), preferred_element_type=jnp.float32)


def dot_tn(a, b):
    return lax.dot_general(a, b, (((0,), (0,)), ((), ())), preferred_element_type=jnp.float32)


def places(group, count):
    first, second = group * 512, (1 - group) * 512
    if count == 4:
        rows = [first, first + 256, second, second + 256]
    else:
        rows = [first, first + 256, 384, second, second + 256, 896]
    return [pl.multiple_of(r, 128) for r in rows]


def stream(weights, pos, held, sems):
    started = {}
    for i in range(4):
        for w, pieces in enumerate(weights):
            piece = pieces[i]
            if isinstance(piece, list):
                parts = []
                for j, (chunk, at) in enumerate(zip(piece, places(pos[1], len(piece)))):
                    size = 128 if len(piece) == 6 and j % 3 else 256
                    source = chunk
                    if j == 5:
                        source = chunk.at[pl.ds(128, 128)]
                    elif len(piece) == 6 and j == 2:
                        source = chunk.at[pl.ds(0, 128)]
                    parts.append((source, held.at[w, i, pl.ds(at, size)], sems.at[w, i, j]))
            else:
                parts = [(piece, held.at[w, i], sems.at[w, i, 0])]
            started[w, i] = [pltpu.make_async_copy(*part) for part in parts]
            for copy in started[w, i]:
                copy.start()

    def ready(w, i):
        for copy in started[w, i]:
            copy.wait()
        return held.at[w, i]

    return ready


TILES = [pl.ds(256 * t, 256) for t in range(4)]


def project_kernel(weights, pos, dense, out, held, sems):
    ready = stream(weights, pos, held, sems)
    totals = [0.0] * 4
    for i in range(4):
        block = ready(0, i)
        rows = dense[0][pos[0] ^ i]
        for t, tile in enumerate(TILES):
            totals[t] += dot_nn(rows, block[:, tile])
    for total, tile in zip(totals, TILES):
        out[:, tile] = total.astype(out.dtype)


def project_out_kernel(weights, pos, dense, out, held, sems):
    ready = stream(weights, pos, held, sems)
    totals = [0.0] * 4
    for i in range(4):
        block = ready(0, i)
        rows = dense[0][pos[0] ^ i]
        for t, tile in enumerate(TILES):
            totals[t] += dot_nt(rows, block[tile])
    for total, tile in zip(totals, TILES):
        out[:, tile] = total.astype(out.dtype)


def emit_kernel(weights, pos, dense, out, held, sems):
    ready = stream(weights, pos, held, sems)
    rows = dense[0][...]
    for i in range(4):
        block = ready(0, i)
        for tile in TILES:
            out[pos[0] ^ i, :, tile] = dot_nn(rows, block[:, tile]).astype(out.dtype)


def back_kernel(weights, pos, dense, out, held, sems):
    ready = stream(weights, pos, held, sems)
    grads = [d[...] for d in dense]
    for i in range(4):
        blocks = [ready(w, i) for w in range(3)]
        for tile in TILES:
            total = sum(dot_nt(g, block[tile]) for g, block in zip(grads, blocks))
            out[pos[0] ^ i, :, tile] = total.astype(out.dtype)


def call(kernel, pos, dense, weights, out_shape, *earlier):
    flat, tree = jax.tree.flatten(weights)
    count = len(weights)

    def run(pos_ref, *refs):
        dense_refs = refs[: len(dense)]
        weight_refs = jax.tree.unflatten(tree, refs[len(dense) : len(dense) + len(flat)])
        out, held, sems = refs[-3:]
        kernel(weight_refs, pos_ref, dense_refs, out, held, sems)

    size = count * 2**22
    return pl.pallas_call(
        run,
        in_specs=[pl.BlockSpec(memory_space=pltpu.SMEM)]
        + [pl.BlockSpec(memory_space=pltpu.VMEM)] * len(dense)
        + [ANYWHERE] * (len(flat) + len(earlier)),
        out_specs=pl.BlockSpec(memory_space=pltpu.VMEM),
        out_shape=out_shape,
        scratch_shapes=[
            pltpu.VMEM((count, 4, 1024, 1024), jnp.bfloat16),
            pltpu.SemaphoreType.DMA((count, 4, 6)),
        ],
        cost_estimate=LITTLE,
        compiler_params=pltpu.CompilerParams(vmem_limit_bytes=(8 * count + 8) * 2**20),
    )(pos, *dense, *flat, *earlier)


def head_pairs(width):
    return [pl.ds(pair * 128, 128) for pair in range(width // 128)]


def first_head(seq):
    return lax.broadcasted_iota(jnp.int32, (seq, 128), 1) < HD


def split_heads(array):
    first = first_head(array.shape[0])
    mask0 = jnp.where(first, 1.0, 0.0).astype(array.dtype)
    mask1 = jnp.where(first, 0.0, 1.0).astype(array.dtype)
    return jnp.concatenate([array * mask0, array * mask1], axis=0)


def join_heads(both):
    seq = both.shape[0] // 2
    return jnp.where(first_head(seq), both[:seq], both[seq:])


def softmax_pair(scores):
    seq = scores.shape[0]
    probs = []
    for h in range(2):
        s = scores[:, h * seq : (h + 1) * seq]
        e = jnp.exp(s - jnp.max(s, axis=-1, keepdims=True))
        probs.append(e / jnp.sum(e, axis=-1, keepdims=True))
    return probs


def attention_kernel(q_ref, k_ref, v_ref, ctx_ref):
    for at in head_pairs(q_ref.shape[1]):
        probs = softmax_pair(dot_nt(q_ref[:, at], split_heads(k_ref[:, at])))
        low = jnp.concatenate([p.astype(jnp.bfloat16) for p in probs], axis=1)
        ctx_ref[:, at] = dot_nn(low, split_heads(v_ref[:, at])).astype(jnp.bfloat16)


def attention_back_kernel(q_ref, k_ref, v_ref, dc_ref, dq_ref, dk_ref, dv_ref):
    seq = q_ref.shape[0]
    for at in head_pairs(q_ref.shape[1]):
        q, dc = q_ref[:, at], dc_ref[:, at]
        keys = split_heads(k_ref[:, at])
        probs = softmax_pair(dot_nt(q, keys))
        d_probs = dot_nt(dc, split_heads(v_ref[:, at]))
        d_scores = []
        for h in range(2):
            dp = d_probs[:, h * seq : (h + 1) * seq]
            ds = probs[h] * (dp - jnp.sum(dp * probs[h], axis=-1, keepdims=True))
            d_scores.append(ds.astype(jnp.bfloat16))
        low = jnp.concatenate([p.astype(jnp.bfloat16) for p in probs], axis=1)
        ds = jnp.concatenate(d_scores, axis=1)
        dq_ref[:, at] = dot_nn(ds, keys).astype(jnp.bfloat16)
        dv_ref[:, at] = join_heads(dot_tn(low, dc)).astype(jnp.bfloat16)
        dk_ref[:, at] = join_heads(dot_tn(ds, q)).astype(jnp.bfloat16)


def attend(kernel, arrays, outputs):
    rows, cols = arrays[0].shape
    spec = pl.BlockSpec((rows // BAL, cols // 2), lambda i, j: (i, j))
    shape = jax.ShapeDtypeStruct((rows, cols), jnp.bfloat16)
    many = len(arrays) + outputs
    return pl.pallas_call(
        kernel,
        grid=(BAL, 2),
        in_specs=[spec] * len(arrays),
        out_specs=[spec] * outputs,
        out_shape=[shape] * outputs,
        cost_estimate=LITTLE,
        compiler_params=pltpu.CompilerParams(vmem_limit_bytes=VMEM_LIMIT),
    )(*arrays)


def cut(weight, block, rows, earlier):
    def copy(block_ref, source, *refs):
        refs[-1][...] = source[...]

    return pl.pallas_call(
        copy,
        grid_spec=pltpu.PrefetchScalarGridSpec(
            num_scalar_prefetch=1,
            grid=(1,),
            in_specs=[pl.BlockSpec((rows, 1024), lambda i, block: (block[0], 0))]
            + [ANYWHERE] * len(earlier),
            out_specs=pl.BlockSpec((rows, 1024), lambda i, block: (0, 0)),
        ),
        out_shape=jax.ShapeDtypeStruct((rows, 1024), weight.dtype),
        cost_estimate=LITTLE,
    )(block.reshape(1), weight, *earlier)


def cut_ends(weight, earlier):
    def copy(low, high, *refs):
        refs[-1][0:128] = low[...]
        refs[-1][128:256] = high[...]

    return pl.pallas_call(
        copy,
        grid=(1,),
        in_specs=[
            pl.BlockSpec((128, 1024), lambda i: (3, 0)),
            pl.BlockSpec((128, 1024), lambda i: (7, 0)),
        ]
        + [ANYWHERE] * len(earlier),
        out_specs=pl.BlockSpec((256, 1024), lambda i: (0, 0)),
        out_shape=jax.ShapeDtypeStruct((256, 1024), weight.dtype),
        cost_estimate=LITTLE,
    )(weight, weight, *earlier)


def finish(d_part, tokens, grads, inverse, row_mean, gain, *earlier):
    def kernel(d_ref, x_ref, g_ref, inverse_ref, mean_ref, gain_ref, *refs):
        d = d_ref[...].astype(jnp.float32)
        scale = inverse_ref[...]
        unit = x_ref[...].astype(jnp.float32) * scale
        d_tokens = scale * (d * gain_ref[...] - unit * mean_ref[...])
        refs[-1][...] = (g_ref[...].astype(jnp.float32) + d_tokens).astype(grads.dtype)

    return pl.pallas_call(
        kernel,
        in_specs=[pl.BlockSpec(memory_space=pltpu.VMEM)] * 6 + [ANYWHERE] * len(earlier),
        out_specs=pl.BlockSpec(memory_space=pltpu.VMEM),
        out_shape=jax.ShapeDtypeStruct(grads.shape, grads.dtype),
        cost_estimate=LITTLE,
        compiler_params=pltpu.CompilerParams(vmem_limit_bytes=VMEM_LIMIT),
    )(d_part, tokens, grads, inverse, row_mean, gain, *earlier)


def after(array, *earlier):
    def nothing(*refs):
        pass

    return pl.pallas_call(
        nothing,
        in_specs=[ANYWHERE] * (1 + len(earlier)),
        out_specs=ANYWHERE,
        out_shape=jax.ShapeDtypeStruct(array.shape, array.dtype),
        input_output_aliases={0: 0},
    )(array, *earlier)


def far_block(chunks, group):
    low, high = jnp.concatenate(chunks[:2]), jnp.concatenate(chunks[2:])
    return jnp.where(group == 0, jnp.concatenate([low, high]), jnp.concatenate([high, low]))


def fast_body(passages, cotangent, passage_counts, norm_gain, w_query, w_key, w_value, w_out):
    me = lax.axis_index("pas")
    group = lax.axis_index("grp")
    feature = lax.axis_index("fsdp")
    seq = passages.shape[1]
    pos = jnp.stack([me, group]).astype(jnp.int32)

    first_chunk = cut(w_key, group * 2, 256, ())

    counts = lax.all_gather(after(passage_counts, first_chunk), "pas", axis=0, tiled=True)
    index = jnp.arange(4, dtype=jnp.int32)
    single = counts == 1
    source = jnp.sum(jnp.where(counts == 4, index, 0))
    rank = lambda d: jnp.minimum(jnp.sum((single & (index < d)).astype(jnp.int32)), 1)
    host0 = jnp.min(jnp.where(single, index, 4))
    host1 = jnp.max(jnp.where(single, index, -1))
    own_count = passage_counts[0]
    relation = me ^ source

    def send_second(array):
        extra = array[2:4]
        extra_core = swap(extra, "pas", 1)
        there = rank(me ^ 2)
        picked = jnp.where(source == me, extra, extra_core)
        return extra_core, jnp.where(there == 0, picked[0], picked[1])

    def second(array, extra_core, got_x):
        from_core = jnp.where(rank(me) == 0, extra_core[0], extra_core[1])
        foreign = jnp.where(relation == 1, from_core, got_x)
        return jnp.where(own_count >= 2, array[1], foreign)

    weights = (w_key, w_query, w_value, w_out)
    over_x, over_y, cuts = [], [], []

    def send(*earlier):
        i = len(over_x)
        if i == 8:
            chunk = cut_ends(w_out, earlier)
        elif i == 7:
            chunk = cut(w_out, group * 4 + 2, 128, earlier)
        elif i == 0:
            chunk = first_chunk
        else:
            chunk = cut(weights[i // 2], group * 2 + i % 2, 256, earlier)
        cuts.append(chunk)
        over_x.append(swap(chunk, "pas", 2))

    def forward(*earlier):
        i = len(over_y)
        if earlier:
            over_x[i] = after(over_x[i], *earlier)
        over_y.append(swap(over_x[i], "grp", 1))

    def fetch(i):
        far = far_block(over_x[i : i + 2] + over_y[i : i + 2], group)
        return [weights[i // 2], swap(weights[i // 2], "pas", 1), far, swap(far, "pas", 1)]

    send()
    tokens_core, tokens_sent = send_second(passages)
    grads_core, grads_sent = send_second(cotangent)
    tokens_x = swap(tokens_sent, "pas", 2)
    grads_x = swap(grads_sent, "pas", 2)
    tokens = jnp.concatenate([passages[0], second(passages, tokens_core, tokens_x)], axis=0)
    send(tokens_sent)
    tokens = after(tokens, cuts[1])
    grads = jnp.concatenate([cotangent[0], second(cotangent, grads_core, grads_x)], axis=0)
    all_tokens = lax.all_gather(tokens, "fsdp", axis=0)
    all_grads = lax.all_gather(grads, "fsdp", axis=0)

    tokens_f32 = all_tokens.astype(jnp.float32)
    width = norm_gain.shape[0]
    gain = norm_gain.reshape(4, 1, 1024)
    inverse = lax.rsqrt(
        jnp.sum(tokens_f32 * tokens_f32, axis=(0, 2), keepdims=True) / width + EPSILON
    )
    normed = (tokens_f32 * inverse * gain).astype(jnp.bfloat16)

    rows_shape = jax.ShapeDtypeStruct((2 * seq, 1024), jnp.bfloat16)
    wide_shape = jax.ShapeDtypeStruct((4, 2 * seq, 1024), jnp.bfloat16)

    def project(w, *earlier):
        return call(project_kernel, pos, [normed], [w], rows_shape, *earlier)

    send(over_x[0], tokens_x)
    forward(cuts[2])
    send(over_x[1], grads_sent)
    forward(cuts[3])
    key_w = fetch(0)
    send(over_x[2], over_y[0])
    forward(cuts[4])
    send(over_x[3], over_y[1], grads)
    forward(cuts[5])
    query_w = fetch(2)
    send(over_x[4], over_y[2])
    forward(cuts[6])
    send(over_x[5], over_y[3])
    forward(cuts[7])
    send(over_x[6], over_y[4])
    keys = project(key_w)
    forward(cuts[8], keys)
    query = project(query_w, all_grads)
    over_x[8] = after(over_x[8], over_y[5], query)
    forward()
    far = over_x[4:6] + over_y[4:6]
    value_w = [w_value, swap(w_value, "pas", 1), far, [swap(c, "pas", 1) for c in far]]
    far = over_x[6:9] + over_y[6:8]
    far_core = [swap(c, "pas", 1) for c in far]
    out_w = [w_out, swap(w_out, "pas", 1), far + far[2:3], far_core + far_core[2:3]]
    values = project(value_w)
    (context,) = attend(attention_kernel, (query, keys, values), 1)
    partial_out = call(emit_kernel, pos, [context], [out_w], wide_shape)
    attention = lax.psum_scatter(partial_out, "fsdp", scatter_dimension=0)
    d_context = call(project_out_kernel, pos, [after(all_grads, partial_out)], [out_w], rows_shape)
    d_query, d_keys, d_values = attend(attention_back_kernel, (query, keys, values, d_context), 3)
    d_normed = call(
        back_kernel, pos, [d_query, d_keys, d_values], [query_w, key_w, value_w], wide_shape
    )

    d_normed = after(d_normed, attention)
    d_part = lax.psum_scatter(d_normed, "fsdp", scatter_dimension=0)

    terms = d_normed.astype(jnp.float32) * (tokens_f32 * inverse)
    row_total = jnp.sum(terms * gain, axis=(0, 2)).reshape(2, seq)
    gain_total = jnp.sum(terms, axis=1).reshape(32, 128)
    for bit in (1, 2):
        row_total += swap(row_total, "fsdp", bit)
        gain_total += swap(gain_total, "fsdp", bit)
    gain_grad = lax.dynamic_slice_in_dim(gain_total, feature * 8, 8, 0)
    for bit in (1, 2):
        gain_grad += swap(gain_grad, "pas", bit)
    row_mean = row_total.reshape(2 * seq, 1) / width

    gain_part = lax.dynamic_slice_in_dim(norm_gain, feature * 1024, 1024, 0)
    states = (tokens.astype(jnp.float32) + attention.reshape(2 * seq, 1024).astype(jnp.float32)).astype(jnp.bfloat16)
    def home(local):
        local = local.reshape(2, seq, 1024)
        back = local[1]
        over_x = swap(back, "pas", 2)
        over_core = swap(back, "pas", 1)
        over_both = swap(over_x, "pas", 1)

        def pick(host):
            way = host ^ me
            return jnp.where(way == 1, over_core, jnp.where(way == 2, over_x, over_both))

        zero = jnp.zeros_like(back)
        return jnp.stack(
            [
                local[0],
                jnp.where(own_count >= 2, back, zero),
                jnp.where(own_count == 4, pick(host0), zero),
                jnp.where(own_count == 4, pick(host1), zero),
            ]
        )

    encoded = home(states)
    input_local = finish(
        d_part.reshape(2 * seq, 1024),
        tokens,
        grads,
        inverse.reshape(2 * seq, 1),
        row_mean,
        gain_part.reshape(1, 1024),
        encoded,
        gain_grad,
    )
    input_grad = home(input_local)
    return encoded, input_grad, gain_grad.reshape(1024)


def solution(mesh):
    placed = (
        P(("grp", "pas"), None, "fsdp"),
        P(("grp", "pas"), None, "fsdp"),
        P(("grp", "pas")),
        P(),
        P("pas", "fsdp"),
        P("pas", "fsdp"),
        P("pas", "fsdp"),
        P("fsdp", "pas"),
    )
    sizes = dict(mesh.shape)
    fast = sizes["grp"] == 2 and sizes["pas"] == 4 and sizes["fsdp"] == 4
    return jax.shard_map(
        fast_body if fast else general_body,
        mesh=mesh,
        in_specs=placed,
        out_specs=(
            P(("grp", "pas"), None, "fsdp"),
            P(("grp", "pas"), None, "fsdp"),
            P(("grp", "fsdp")),
        ),
        check_vma=False,
    )
```

```python
import jax
import jax.numpy as jnp
from jax import lax
from jax.experimental import pallas as pl
from jax.experimental.pallas import tpu as pltpu
from jax.sharding import PartitionSpec as P

HD = 64
BAL = 2
EPSILON = 1e-06
VMEM_LIMIT = 50 * 2**20
LITTLE = pl.CostEstimate(flops=1, bytes_accessed=1, transcendentals=0)


def entering(shard, axis, combine, identity):
    length, position = (lax.axis_size(axis), lax.axis_index(axis))
    everything = lax.all_gather(shard, axis)
    start = jnp.broadcast_to(jnp.asarray(identity, shard.dtype), shard.shape)

    def lap(k, before):
        reached = k < position
        new = combine(before, everything[k])
        return jnp.where(reached, new, before)

    return lax.fori_loop(0, length, lap, start)


def add_counts(earlier, later):
    return earlier + later


def general_body(passages, cotangent, passage_counts, norm_gain, w_query, w_key, w_value, w_out):
    peer_total = lax.axis_size("pas")
    slots, seq_len, part_width = passages.shape
    flat_width = seq_len * part_width
    own_count = passage_counts[0]
    first_rank = entering(passage_counts, "pas", add_counts, jnp.zeros_like(passage_counts))[0]
    slot_index = jnp.arange(slots, dtype=jnp.int32)
    slot_rank = first_rank + slot_index
    is_live = slot_index < own_count
    peer_index = jnp.arange(peer_total, dtype=jnp.int32)
    routing_mask = is_live[None, :] & ((slot_rank % peer_total)[None, :] == peer_index[:, None])
    routing = routing_mask.astype(jnp.bfloat16)
    sent_rank = jnp.max(jnp.where(routing_mask, slot_rank[None, :], -1), axis=1).astype(jnp.int32)
    send_tokens = jnp.dot(
        routing, passages.reshape(slots, flat_width), preferred_element_type=jnp.float32
    ).astype(jnp.bfloat16)
    send_grads = jnp.dot(
        routing, cotangent.reshape(slots, flat_width), preferred_element_type=jnp.float32
    ).astype(jnp.bfloat16)
    got_tokens, got_grads, got_rank = (
        lax.all_to_all(send_tokens, "pas", split_axis=0, concat_axis=0, tiled=True),
        lax.all_to_all(send_grads, "pas", split_axis=0, concat_axis=0, tiled=True),
        lax.all_to_all(sent_rank, "pas", split_axis=0, concat_axis=0, tiled=True),
    )
    picked_mask = (got_rank[None, :] >= 0) & (
        got_rank[None, :] // peer_total == jnp.arange(BAL, dtype=jnp.int32)[:, None]
    )
    picked = picked_mask.astype(jnp.bfloat16)
    returned = jnp.transpose(picked)
    local_tokens = (
        jnp.dot(picked, got_tokens, preferred_element_type=jnp.float32)
        .astype(jnp.bfloat16)
        .reshape(BAL, seq_len, part_width)
    )
    local_grads = (
        jnp.dot(picked, got_grads, preferred_element_type=jnp.float32)
        .astype(jnp.bfloat16)
        .reshape(BAL, seq_len, part_width)
    )
    query_w, key_w, value_w, out_w = (
        lax.all_gather(w_query, "pas", axis=0, tiled=True),
        lax.all_gather(w_key, "pas", axis=0, tiled=True),
        lax.all_gather(w_value, "pas", axis=0, tiled=True),
        lax.all_gather(w_out, "pas", axis=1, tiled=True),
    )
    full_tokens = lax.all_gather(local_tokens, "fsdp", axis=2, tiled=True)
    width = full_tokens.shape[2]
    feature_start = lax.axis_index("fsdp") * part_width
    full_f32 = full_tokens.astype(jnp.float32)
    inverse = lax.rsqrt(jnp.mean(full_f32 * full_f32, axis=-1, keepdims=True) + EPSILON)
    unit_rows = full_f32 * inverse
    normed = (unit_rows * norm_gain).astype(jnp.bfloat16)
    local_cols = query_w.shape[1]
    head_count = local_cols // HD
    flat_rows = normed.reshape(BAL * seq_len, width)

    def project(weight):
        result = jnp.dot(flat_rows, weight, preferred_element_type=jnp.float32).astype(jnp.bfloat16)
        return result.reshape(BAL, seq_len, head_count, HD)

    query = project(query_w)
    keys = project(key_w)
    values = project(value_w)
    scores = jnp.einsum("blhe,bmhe->bhlm", query, keys, preferred_element_type=jnp.float32)
    probs = jax.nn.softmax(scores, axis=-1)
    probs_low = probs.astype(jnp.bfloat16)
    context = jnp.einsum(
        "bhlm,bmhe->blhe", probs_low, values, preferred_element_type=jnp.float32
    ).astype(jnp.bfloat16)
    context_rows = context.reshape(BAL * seq_len, local_cols)
    partial_out = jnp.dot(context_rows, out_w, preferred_element_type=jnp.float32).reshape(
        BAL, seq_len, width
    )
    attention = lax.psum_scatter(
        partial_out.astype(jnp.bfloat16), "fsdp", scatter_dimension=2, tiled=True
    ).astype(jnp.float32)
    states = (local_tokens.astype(jnp.float32) + attention).astype(jnp.bfloat16)
    states_back = jnp.dot(
        returned, states.reshape(BAL, flat_width), preferred_element_type=jnp.float32
    ).astype(jnp.bfloat16)
    states_home = lax.all_to_all(states_back, "pas", split_axis=0, concat_axis=0, tiled=True)
    upstream_rows = lax.all_gather(local_grads, "fsdp", axis=2, tiled=True).reshape(
        BAL * seq_len, width
    )
    d_context = jnp.einsum(
        "td,cd->tc", upstream_rows, out_w, preferred_element_type=jnp.float32
    ).astype(jnp.bfloat16)
    d_context = d_context.reshape(BAL, seq_len, head_count, HD)
    d_values = jnp.einsum(
        "bhlm,blhe->bmhe", probs_low, d_context, preferred_element_type=jnp.float32
    ).astype(jnp.bfloat16)
    d_probs = jnp.einsum("blhe,bmhe->bhlm", d_context, values, preferred_element_type=jnp.float32)
    d_scores = (probs * (d_probs - jnp.sum(d_probs * probs, axis=-1, keepdims=True))).astype(
        jnp.bfloat16
    )
    d_query = jnp.einsum(
        "bhlm,bmhe->blhe", d_scores, keys, preferred_element_type=jnp.float32
    ).astype(jnp.bfloat16)
    d_keys = jnp.einsum(
        "bhlm,blhe->bmhe", d_scores, query, preferred_element_type=jnp.float32
    ).astype(jnp.bfloat16)

    def back_project(grad, weight):
        grad_rows = grad.reshape(BAL * seq_len, local_cols)
        return jnp.einsum("tc,dc->td", grad_rows, weight, preferred_element_type=jnp.float32)

    d_normed = (
        back_project(d_query, query_w)
        + back_project(d_keys, key_w)
        + back_project(d_values, value_w)
    )
    d_normed_part = lax.psum_scatter(
        d_normed.reshape(BAL, seq_len, width).astype(jnp.bfloat16),
        "fsdp",
        scatter_dimension=2,
        tiled=True,
    ).astype(jnp.float32)
    unit_part = lax.dynamic_slice_in_dim(unit_rows, feature_start, part_width, 2)
    gain_part = lax.dynamic_slice_in_dim(norm_gain, feature_start, part_width, 0)
    d_unit = d_normed_part * gain_part
    row_total = lax.psum(jnp.sum(d_unit * unit_part, axis=-1, keepdims=True), "fsdp")
    row_mean = row_total / width
    d_tokens = inverse * (d_unit - unit_part * row_mean)
    grads_local = (local_grads.astype(jnp.float32) + d_tokens).astype(jnp.bfloat16)
    gain_grad = lax.psum(jnp.sum(d_normed_part * unit_part, axis=(0, 1)), "pas")
    grads_back = jnp.dot(
        returned, grads_local.reshape(BAL, flat_width), preferred_element_type=jnp.float32
    ).astype(jnp.bfloat16)
    grads_home = lax.all_to_all(grads_back, "pas", split_axis=0, concat_axis=0, tiled=True)
    routing_back = jnp.transpose(routing)
    encoded = (
        jnp.dot(routing_back, states_home, preferred_element_type=jnp.float32)
        .astype(jnp.bfloat16)
        .reshape(slots, seq_len, part_width)
    )
    input_grad = (
        jnp.dot(routing_back, grads_home, preferred_element_type=jnp.float32)
        .astype(jnp.bfloat16)
        .reshape(slots, seq_len, part_width)
    )
    return (encoded, input_grad, gain_grad)


ANYWHERE = pl.BlockSpec(memory_space=pl.ANY)


def swap(array, axis, bit):
    return lax.ppermute(array, axis, [(i, i ^ bit) for i in range(lax.axis_size(axis))])


def dot_nn(a, b):
    return jnp.dot(a, b, preferred_element_type=jnp.float32)


def dot_nt(a, b):
    return lax.dot_general(a, b, (((1,), (1,)), ((), ())), preferred_element_type=jnp.float32)


def dot_tn(a, b):
    return lax.dot_general(a, b, (((0,), (0,)), ((), ())), preferred_element_type=jnp.float32)


def places(group, count):
    first, second = group * 512, (1 - group) * 512
    if count == 4:
        rows = [first, first + 256, second, second + 256]
    else:
        rows = [first, first + 256, 384, second, second + 256, 896]
    return [pl.multiple_of(r, 128) for r in rows]


def stream(weights, pos, held, sems):
    started = {}
    for i in range(4):
        for w, pieces in enumerate(weights):
            piece = pieces[i]
            if isinstance(piece, list):
                parts = []
                for j, (chunk, at) in enumerate(zip(piece, places(pos[1], len(piece)))):
                    size = 128 if len(piece) == 6 and j % 3 else 256
                    source = chunk
                    if j == 5:
                        source = chunk.at[pl.ds(128, 128)]
                    elif len(piece) == 6 and j == 2:
                        source = chunk.at[pl.ds(0, 128)]
                    parts.append((source, held.at[w, i, pl.ds(at, size)], sems.at[w, i, j]))
            else:
                parts = [(piece, held.at[w, i], sems.at[w, i, 0])]
            started[w, i] = [pltpu.make_async_copy(*part) for part in parts]
            for copy in started[w, i]:
                copy.start()

    def ready(w, i):
        for copy in started[w, i]:
            copy.wait()
        return held.at[w, i]

    return ready


TILES = [pl.ds(256 * t, 256) for t in range(4)]


def project_kernel(weights, pos, dense, out, held, sems):
    ready = stream(weights, pos, held, sems)
    totals = [0.0] * 4
    for i in range(4):
        block = ready(0, i)
        rows = dense[0][pos[0] ^ i]
        for t, tile in enumerate(TILES):
            totals[t] += dot_nn(rows, block[:, tile])
    for total, tile in zip(totals, TILES):
        out[:, tile] = total.astype(out.dtype)


def project_out_kernel(weights, pos, dense, out, held, sems):
    ready = stream(weights, pos, held, sems)
    totals = [0.0] * 4
    for i in range(4):
        block = ready(0, i)
        rows = dense[0][pos[0] ^ i]
        for t, tile in enumerate(TILES):
            totals[t] += dot_nt(rows, block[tile])
    for total, tile in zip(totals, TILES):
        out[:, tile] = total.astype(out.dtype)


def emit_kernel(weights, pos, dense, out, held, sems, blocks, out_sems):
    ready = stream(weights, pos, held, sems)
    rows = dense[0][...]
    written = []
    for i in range(4):
        block = ready(0, i)
        for tile in TILES:
            blocks[i, :, tile] = dot_nn(rows, block[:, tile]).astype(out.dtype)
        written.append(pltpu.make_async_copy(blocks.at[i], out.at[pos[0] ^ i], out_sems.at[i]))
        written[i].start()
    for copy in written:
        copy.wait()


def back_kernel(weights, pos, dense, out, held, sems):
    ready = stream(weights, pos, held, sems)
    grads = [d[...] for d in dense]
    for i in range(4):
        blocks = [ready(w, i) for w in range(3)]
        for tile in TILES:
            total = sum(dot_nt(g, block[tile]) for g, block in zip(grads, blocks))
            out[pos[0] ^ i, :, tile] = total.astype(out.dtype)


def call(kernel, pos, dense, weights, out_shape, *earlier):
    flat, tree = jax.tree.flatten(weights)
    count = len(weights)
    direct = kernel is emit_kernel
    staging = [pltpu.VMEM(out_shape.shape, out_shape.dtype), pltpu.SemaphoreType.DMA((4,))]

    def run(pos_ref, *refs):
        dense_refs = refs[: len(dense)]
        weight_refs = jax.tree.unflatten(tree, refs[len(dense) : len(dense) + len(flat)])
        own = refs[-5:] if direct else refs[-3:]
        kernel(weight_refs, pos_ref, dense_refs, *own)

    size = count * 2**22
    return pl.pallas_call(
        run,
        in_specs=[pl.BlockSpec(memory_space=pltpu.SMEM)]
        + [pl.BlockSpec(memory_space=pltpu.VMEM)] * len(dense)
        + [ANYWHERE] * (len(flat) + len(earlier)),
        out_specs=ANYWHERE if direct else pl.BlockSpec(memory_space=pltpu.VMEM),
        out_shape=out_shape,
        scratch_shapes=[
            pltpu.VMEM((count, 4, 1024, 1024), jnp.bfloat16),
            pltpu.SemaphoreType.DMA((count, 4, 6)),
        ]
        + (staging if direct else []),
        cost_estimate=LITTLE,
        compiler_params=pltpu.CompilerParams(vmem_limit_bytes=(8 * count + 8) * 2**20),
    )(pos, *dense, *flat, *earlier)


def head_pairs(width):
    return [pl.ds(pair * 128, 128) for pair in range(width // 128)]


def first_head(seq):
    return lax.broadcasted_iota(jnp.int32, (seq, 128), 1) < HD


def split_heads(array):
    first = first_head(array.shape[0])
    mask0 = jnp.where(first, 1.0, 0.0).astype(array.dtype)
    mask1 = jnp.where(first, 0.0, 1.0).astype(array.dtype)
    return jnp.concatenate([array * mask0, array * mask1], axis=0)


def join_heads(both):
    seq = both.shape[0] // 2
    return jnp.where(first_head(seq), both[:seq], both[seq:])


def softmax_pair(scores):
    seq = scores.shape[0]
    probs = []
    for h in range(2):
        s = scores[:, h * seq : (h + 1) * seq]
        e = jnp.exp(s - jnp.max(s, axis=-1, keepdims=True))
        probs.append(e / jnp.sum(e, axis=-1, keepdims=True))
    return probs


def attention_kernel(q_ref, k_ref, v_ref, ctx_ref):
    for at in head_pairs(q_ref.shape[1]):
        probs = softmax_pair(dot_nt(q_ref[:, at], split_heads(k_ref[:, at])))
        low = jnp.concatenate([p.astype(jnp.bfloat16) for p in probs], axis=1)
        ctx_ref[:, at] = dot_nn(low, split_heads(v_ref[:, at])).astype(jnp.bfloat16)


def attention_back_kernel(q_ref, k_ref, v_ref, dc_ref, dq_ref, dk_ref, dv_ref):
    seq = q_ref.shape[0]
    for at in head_pairs(q_ref.shape[1]):
        q, dc = q_ref[:, at], dc_ref[:, at]
        keys = split_heads(k_ref[:, at])
        probs = softmax_pair(dot_nt(q, keys))
        d_probs = dot_nt(dc, split_heads(v_ref[:, at]))
        d_scores = []
        for h in range(2):
            dp = d_probs[:, h * seq : (h + 1) * seq]
            ds = probs[h] * (dp - jnp.sum(dp * probs[h], axis=-1, keepdims=True))
            d_scores.append(ds.astype(jnp.bfloat16))
        low = jnp.concatenate([p.astype(jnp.bfloat16) for p in probs], axis=1)
        ds = jnp.concatenate(d_scores, axis=1)
        dq_ref[:, at] = dot_nn(ds, keys).astype(jnp.bfloat16)
        dv_ref[:, at] = join_heads(dot_tn(low, dc)).astype(jnp.bfloat16)
        dk_ref[:, at] = join_heads(dot_tn(ds, q)).astype(jnp.bfloat16)


def attend(kernel, arrays, outputs):
    rows, cols = arrays[0].shape
    spec = pl.BlockSpec((rows // BAL, cols // 2), lambda i, j: (i, j))
    shape = jax.ShapeDtypeStruct((rows, cols), jnp.bfloat16)
    many = len(arrays) + outputs
    return pl.pallas_call(
        kernel,
        grid=(BAL, 2),
        in_specs=[spec] * len(arrays),
        out_specs=[spec] * outputs,
        out_shape=[shape] * outputs,
        cost_estimate=LITTLE,
        compiler_params=pltpu.CompilerParams(vmem_limit_bytes=VMEM_LIMIT),
    )(*arrays)


def cut(weight, block, rows, earlier):
    def copy(block_ref, source, *refs):
        refs[-1][...] = source[...]

    return pl.pallas_call(
        copy,
        grid_spec=pltpu.PrefetchScalarGridSpec(
            num_scalar_prefetch=1,
            grid=(1,),
            in_specs=[pl.BlockSpec((rows, 1024), lambda i, block: (block[0], 0))]
            + [ANYWHERE] * len(earlier),
            out_specs=pl.BlockSpec((rows, 1024), lambda i, block: (0, 0)),
        ),
        out_shape=jax.ShapeDtypeStruct((rows, 1024), weight.dtype),
        cost_estimate=LITTLE,
    )(block.reshape(1), weight, *earlier)


def cut_ends(weight, earlier):
    def copy(low, high, *refs):
        refs[-1][0:128] = low[...]
        refs[-1][128:256] = high[...]

    return pl.pallas_call(
        copy,
        grid=(1,),
        in_specs=[
            pl.BlockSpec((128, 1024), lambda i: (3, 0)),
            pl.BlockSpec((128, 1024), lambda i: (7, 0)),
        ]
        + [ANYWHERE] * len(earlier),
        out_specs=pl.BlockSpec((256, 1024), lambda i: (0, 0)),
        out_shape=jax.ShapeDtypeStruct((256, 1024), weight.dtype),
        cost_estimate=LITTLE,
    )(weight, weight, *earlier)


def finish(d_part, tokens, grads, inverse, row_mean, gain, *earlier):
    def kernel(d_ref, x_ref, g_ref, inverse_ref, mean_ref, gain_ref, *refs):
        d = d_ref[...].astype(jnp.float32)
        scale = inverse_ref[...]
        unit = x_ref[...].astype(jnp.float32) * scale
        d_tokens = scale * (d * gain_ref[...] - unit * mean_ref[...])
        refs[-1][...] = (g_ref[...].astype(jnp.float32) + d_tokens).astype(grads.dtype)

    return pl.pallas_call(
        kernel,
        in_specs=[pl.BlockSpec(memory_space=pltpu.VMEM)] * 6 + [ANYWHERE] * len(earlier),
        out_specs=pl.BlockSpec(memory_space=pltpu.VMEM),
        out_shape=jax.ShapeDtypeStruct(grads.shape, grads.dtype),
        cost_estimate=LITTLE,
        compiler_params=pltpu.CompilerParams(vmem_limit_bytes=VMEM_LIMIT),
    )(d_part, tokens, grads, inverse, row_mean, gain, *earlier)


def after(array, *earlier):
    def nothing(*refs):
        pass

    return pl.pallas_call(
        nothing,
        in_specs=[ANYWHERE] * (1 + len(earlier)),
        out_specs=ANYWHERE,
        out_shape=jax.ShapeDtypeStruct(array.shape, array.dtype),
        input_output_aliases={0: 0},
    )(array, *earlier)


def far_block(chunks, group):
    low, high = jnp.concatenate(chunks[:2]), jnp.concatenate(chunks[2:])
    return jnp.where(group == 0, jnp.concatenate([low, high]), jnp.concatenate([high, low]))


def fast_body(passages, cotangent, passage_counts, norm_gain, w_query, w_key, w_value, w_out):
    me = lax.axis_index("pas")
    group = lax.axis_index("grp")
    feature = lax.axis_index("fsdp")
    seq = passages.shape[1]
    pos = jnp.stack([me, group]).astype(jnp.int32)

    first_chunk = cut(w_key, group * 2, 256, ())

    counts = lax.all_gather(after(passage_counts, first_chunk), "pas", axis=0, tiled=True)
    index = jnp.arange(4, dtype=jnp.int32)
    single = counts == 1
    source = jnp.sum(jnp.where(counts == 4, index, 0))
    rank = lambda d: jnp.minimum(jnp.sum((single & (index < d)).astype(jnp.int32)), 1)
    host0 = jnp.min(jnp.where(single, index, 4))
    host1 = jnp.max(jnp.where(single, index, -1))
    own_count = passage_counts[0]
    relation = me ^ source

    def send_second(array):
        extra = array[2:4]
        extra_core = swap(extra, "pas", 1)
        there = rank(me ^ 2)
        picked = jnp.where(source == me, extra, extra_core)
        return extra_core, jnp.where(there == 0, picked[0], picked[1])

    def second(array, extra_core, got_x):
        from_core = jnp.where(rank(me) == 0, extra_core[0], extra_core[1])
        foreign = jnp.where(relation == 1, from_core, got_x)
        return jnp.where(own_count >= 2, array[1], foreign)

    weights = (w_key, w_query, w_value, w_out)
    over_x, over_y, cuts = [], [], []

    def send(*earlier):
        i = len(over_x)
        if i == 8:
            chunk = cut_ends(w_out, earlier)
        elif i == 7:
            chunk = cut(w_out, group * 4 + 2, 128, earlier)
        elif i == 0:
            chunk = first_chunk
        else:
            chunk = cut(weights[i // 2], group * 2 + i % 2, 256, earlier)
        cuts.append(chunk)
        over_x.append(swap(chunk, "pas", 2))

    def forward(*earlier):
        i = len(over_y)
        if earlier:
            over_x[i] = after(over_x[i], *earlier)
        over_y.append(swap(over_x[i], "grp", 1))

    def fetch(i):
        far = far_block(over_x[i : i + 2] + over_y[i : i + 2], group)
        return [weights[i // 2], swap(weights[i // 2], "pas", 1), far, swap(far, "pas", 1)]

    send()
    tokens_core, tokens_sent = send_second(passages)
    grads_core, grads_sent = send_second(cotangent)
    tokens_x = swap(tokens_sent, "pas", 2)
    grads_x = swap(grads_sent, "pas", 2)
    tokens = jnp.concatenate([passages[0], second(passages, tokens_core, tokens_x)], axis=0)
    send(tokens_sent)
    tokens = after(tokens, cuts[1])
    grads = jnp.concatenate([cotangent[0], second(cotangent, grads_core, grads_x)], axis=0)
    all_tokens = lax.all_gather(tokens, "fsdp", axis=0)
    all_grads = lax.all_gather(grads, "fsdp", axis=0)

    tokens_f32 = all_tokens.astype(jnp.float32)
    width = norm_gain.shape[0]
    gain = norm_gain.reshape(4, 1, 1024)
    inverse = lax.rsqrt(
        jnp.sum(tokens_f32 * tokens_f32, axis=(0, 2), keepdims=True) / width + EPSILON
    )
    normed = (tokens_f32 * inverse * gain).astype(jnp.bfloat16)

    rows_shape = jax.ShapeDtypeStruct((2 * seq, 1024), jnp.bfloat16)
    wide_shape = jax.ShapeDtypeStruct((4, 2 * seq, 1024), jnp.bfloat16)

    def project(w, *earlier):
        return call(project_kernel, pos, [normed], [w], rows_shape, *earlier)

    send(over_x[0], tokens_x)
    forward(cuts[2])
    send(over_x[1], grads_sent)
    forward(cuts[3])
    key_w = fetch(0)
    send(over_x[2], over_y[0])
    forward(cuts[4])
    send(over_x[3], over_y[1], grads)
    forward(cuts[5])
    query_w = fetch(2)
    send(over_x[4], over_y[2])
    forward(cuts[6])
    send(over_x[5], over_y[3])
    forward(cuts[7])
    send(over_x[6], over_y[4])
    keys = project(key_w)
    forward(cuts[8], keys)
    query = project(query_w, all_grads)
    over_x[8] = after(over_x[8], over_y[5], query)
    forward()
    far = over_x[4:6] + over_y[4:6]
    value_w = [w_value, swap(w_value, "pas", 1), far, [swap(c, "pas", 1) for c in far]]
    far = over_x[6:9] + over_y[6:8]
    far_core = [swap(c, "pas", 1) for c in far]
    out_w = [w_out, swap(w_out, "pas", 1), far + far[2:3], far_core + far_core[2:3]]
    values = project(value_w)
    (context,) = attend(attention_kernel, (query, keys, values), 1)
    partial_out = call(emit_kernel, pos, [context], [out_w], wide_shape)
    attention = lax.psum_scatter(partial_out, "fsdp", scatter_dimension=0)
    d_context = call(project_out_kernel, pos, [after(all_grads, partial_out)], [out_w], rows_shape)
    d_query, d_keys, d_values = attend(attention_back_kernel, (query, keys, values, d_context), 3)
    d_normed = call(
        back_kernel, pos, [d_query, d_keys, d_values], [query_w, key_w, value_w], wide_shape
    )

    d_normed = after(d_normed, attention)
    d_part = lax.psum_scatter(d_normed, "fsdp", scatter_dimension=0)

    terms = d_normed.astype(jnp.float32) * (tokens_f32 * inverse)
    row_total = jnp.sum(terms * gain, axis=(0, 2)).reshape(2, seq)
    gain_total = jnp.sum(terms, axis=1).reshape(32, 128)
    for bit in (1, 2):
        row_total += swap(row_total, "fsdp", bit)
        gain_total += swap(gain_total, "fsdp", bit)
    gain_grad = lax.dynamic_slice_in_dim(gain_total, feature * 8, 8, 0)
    for bit in (1, 2):
        gain_grad += swap(gain_grad, "pas", bit)
    row_mean = row_total.reshape(2 * seq, 1) / width

    gain_part = lax.dynamic_slice_in_dim(norm_gain, feature * 1024, 1024, 0)
    states = (tokens.astype(jnp.float32) + attention.reshape(2 * seq, 1024).astype(jnp.float32)).astype(jnp.bfloat16)
    def home(local):
        local = local.reshape(2, seq, 1024)
        back = local[1]
        over_x = swap(back, "pas", 2)
        over_core = swap(back, "pas", 1)
        over_both = swap(over_x, "pas", 1)

        def pick(host):
            way = host ^ me
            return jnp.where(way == 1, over_core, jnp.where(way == 2, over_x, over_both))

        zero = jnp.zeros_like(back)
        return jnp.stack(
            [
                local[0],
                jnp.where(own_count >= 2, back, zero),
                jnp.where(own_count == 4, pick(host0), zero),
                jnp.where(own_count == 4, pick(host1), zero),
            ]
        )

    encoded = home(states)
    input_local = finish(
        d_part.reshape(2 * seq, 1024),
        tokens,
        grads,
        inverse.reshape(2 * seq, 1),
        row_mean,
        gain_part.reshape(1, 1024),
        encoded,
        gain_grad,
    )
    input_grad = home(input_local)
    return encoded, input_grad, gain_grad.reshape(1024)


def solution(mesh):
    placed = (
        P(("grp", "pas"), None, "fsdp"),
        P(("grp", "pas"), None, "fsdp"),
        P(("grp", "pas")),
        P(),
        P("pas", "fsdp"),
        P("pas", "fsdp"),
        P("pas", "fsdp"),
        P("fsdp", "pas"),
    )
    sizes = dict(mesh.shape)
    fast = sizes["grp"] == 2 and sizes["pas"] == 4 and sizes["fsdp"] == 4
    return jax.shard_map(
        fast_body if fast else general_body,
        mesh=mesh,
        in_specs=placed,
        out_specs=(
            P(("grp", "pas"), None, "fsdp"),
            P(("grp", "pas"), None, "fsdp"),
            P(("grp", "fsdp")),
        ),
        check_vma=False,
    )
```
